512 devices in a mesh: depth: 32 (over z, core), lat: 16 (over y, x).
Axes of the slice: x: 4, y: 4, z: 16, core: 2. Of those that a mesh axis runs over, the one named last changes fastest.
Arguments:
- inv_diag: bfloat16 [32, 1024, 1024], P('depth', 'lat'), may hold values from -1.3 to 1.3
- couple: bfloat16 [32, 1024, 1024], P('depth', None, 'lat'), may hold values from -1 to 1
- arrow: bfloat16 [32, 1024, 1024], P('depth', None, 'lat'), may hold values from -6 to 6
- corner: bfloat16 [1024, 1024], replicated, may hold values from -2 to 2, as said below
- band_offset: int32 [32], P('depth'), may hold values from -8 to 8, as said below
Outputs:
- cross_cov: float32 [32, 1024, 1024], P('depth', 'lat')
The draws below stay inside these ranges and needn't reach their ends.
Inputs may be any that keep to these rules, and one draw needn't show every extreme that they name: `band_offset`: each layer's band lies at this shift; both ends of the range occur in every draw. `corner`: Symmetric.
All inputs are finite; a program needn't handle non-finite values.
Results may differ from the reference program's by a relative error of at most 0.035.
Values may be sent and summed in bfloat16 or wider, within the bound.
No kernel may reach another device: no remote copies, remote signals or barrier semaphores. Data moves between devices by JAX's collectives and lax.ppermute only.
A program may use at most 64 MiB of HBM per device.

```python
from functools import partial
import jax
import jax.numpy as jnp
from jax import lax

W = 1024
A = 1024
OFF_MOST = 8
HALF = 512
LAYERS = 32
N_LAT = 16


def band_offsets(key):
    first = jax.random.fold_in(key, 77)
    second = jax.random.fold_in(key, 78)
    shifts = jax.random.randint(first, (LAYERS,), -OFF_MOST, OFF_MOST + 1)
    order = jax.random.permutation(second, LAYERS)
    shifts = shifts.at[order[0]].set(OFF_MOST).at[order[1]].set(-OFF_MOST)
    return shifts.astype(jnp.int32)


def draw_band_offset(key, part):
    return band_offsets(key)


def draw_couple(key, part):
    shifts = band_offsets(key)
    key = jax.random.fold_in(key, 3)
    first, second, third = jax.random.split(key, 3)
    shape = (LAYERS, W, W)
    rows = lax.broadcasted_iota(jnp.int32, shape, 1)
    cols = lax.broadcasted_iota(jnp.int32, shape, 2)
    lead = cols == rows + shifts[:, None, None]
    spread = 0.3 / jnp.sqrt(2.0 * HALF + 1.0)
    base = jax.random.normal(first, shape, jnp.float32) * spread
    base = jnp.clip(base, -0.5, 0.5)
    size = jax.random.uniform(second, shape, jnp.float32, 0.9, 1.0)
    sign = jnp.where(jax.random.bernoulli(third, 0.5, shape), 1.0, -1.0)
    return jnp.where(lead, sign * size, base).astype(jnp.bfloat16)


def draw_inv_diag(key, part):
    key = jax.random.fold_in(key, 5)
    first, second = jax.random.split(key)
    shape = (LAYERS, W, W)
    rows = lax.broadcasted_iota(jnp.int32, shape, 1)
    cols = lax.broadcasted_iota(jnp.int32, shape, 2)
    spread = 0.4 / jnp.sqrt(1.0 * W)
    below = jax.random.normal(first, shape, jnp.float32) * spread
    middle = jax.random.uniform(second, shape, jnp.float32, 0.9, 1.1)
    below = jnp.clip(below, -0.3, 0.3)
    lower = jnp.where(rows > cols, below, 0.0)
    return jnp.where(rows == cols, middle, lower).astype(jnp.bfloat16)


def draw_corner(key, part):
    key = jax.random.fold_in(key, 7)
    first, second = jax.random.split(key)
    shape = (A, A)
    spread = 0.5 / jnp.sqrt(1.0 * A)
    noise = jax.random.normal(first, shape, jnp.float32) * spread
    mixed = jnp.clip((noise + noise.T) * 0.70710678, -0.5, 0.5)
    middle = jax.random.uniform(second, (A,), jnp.float32, 1.0, 2.0)
    rows = lax.broadcasted_iota(jnp.int32, shape, 0)
    cols = lax.broadcasted_iota(jnp.int32, shape, 1)
    return jnp.where(rows == cols, middle[:, None] * jnp.ones_like(mixed), mixed).astype(jnp.bfloat16)


def steps_of(key, extent, pieces, low, high):
    factor_of, own = 1.0, jax.random.fold_in(key, 6)
    for position, blocks in pieces:
        steps = jnp.exp(jax.random.uniform(jax.random.fold_in(own, position), (blocks,), jnp.float32, low / len(pieces), high / len(pieces)))
        factor_of = factor_of * jnp.repeat(steps, extent[position] // blocks).reshape([-1 if axis == position else 1 for axis in range(len(extent))])
    return factor_of


def normal_values(own_key, extent, scale, bound, cuts=(), held_as=jnp.bfloat16):
    drawn = jax.random.normal(own_key, extent, jnp.float32) * scale
    if len(cuts) > 0:
        drawn = steps_of(own_key, extent, cuts, -0.22, 0.18) * drawn
    return jnp.clip(drawn, min=-bound, max=bound).astype(held_as)


def setup_inputs(seed: int = 0) -> dict:
    streams_of = jax.random.split(jax.random.key(seed), 6)
    return {
        "inv_diag": draw_inv_diag(jax.random.fold_in(streams_of[5], 71), 0),
        "couple": draw_couple(jax.random.fold_in(streams_of[5], 71), 0),
        "arrow": normal_values(streams_of[2], (LAYERS, A, W), 1.0, 6.0, ((0, 32), (2, 16))),
        "corner": draw_corner(jax.random.fold_in(streams_of[5], 71), 0),
        "band_offset": draw_band_offset(jax.random.fold_in(streams_of[5], 71), 0),
    }


def block_sum(left, right, blocks):
    rows = left.shape[0]
    inner = left.shape[1]
    wide = right.shape[1]
    left_f = left.astype(jnp.float32).reshape(rows, blocks, inner // blocks)
    right_f = right.astype(jnp.float32).reshape(blocks, inner // blocks, wide)
    parts = jnp.einsum("rbk,bkc->brc", left_f, right_f)
    rounded = lax.optimization_barrier(parts.astype(jnp.bfloat16))
    return jnp.sum(rounded.astype(jnp.float32), axis=0)


def layer_terms(corner_block, items):
    inverse, coupling, arrow_block, offset = items
    rows = lax.broadcasted_iota(jnp.int32, coupling.shape, 0)
    cols = lax.broadcasted_iota(jnp.int32, coupling.shape, 1)
    keep = jnp.abs(cols - rows - offset) <= HALF
    banded = jnp.where(keep, coupling, jnp.zeros_like(coupling))
    step_map = (-block_sum(banded, inverse, N_LAT)).astype(jnp.bfloat16)
    panel = jnp.dot(corner_block, arrow_block, preferred_element_type=jnp.float32).astype(jnp.bfloat16)
    step_bias = -block_sum(panel, inverse, N_LAT)
    return step_map, step_bias


def bias_step(items):
    return jnp.dot(items[0], items[1].astype(jnp.float32), precision=lax.Precision.HIGHEST)


def map_step(items):
    return jnp.dot(items[0], items[1], preferred_element_type=jnp.float32).astype(jnp.bfloat16)


def reference(inv_diag, couple, arrow, corner, band_offset):
    comp_map, comp_bias = lax.map(partial(layer_terms, corner), (inv_diag, couple, arrow, band_offset))
    levels = (LAYERS - 1).bit_length()
    for level in range(levels):
        span = 2 ** level
        bias_partner = jnp.concatenate([comp_bias[span:], jnp.zeros_like(comp_bias[:span])], axis=0)
        new_bias = lax.map(bias_step, (bias_partner, comp_map)) + comp_bias
        if level < levels - 1:
            map_partner = jnp.concatenate([comp_map[span:], jnp.zeros_like(comp_map[:span])], axis=0)
            comp_map = lax.map(map_step, (map_partner, comp_map))
        comp_bias = new_bias
    return comp_bias
```

```python
import jax
import jax.numpy as jnp
from jax import lax
from jax.sharding import PartitionSpec as P

HALF = 512
BOTH = ("depth", "lat")
F32 = jnp.float32
BF16 = jnp.bfloat16


def groups(depth_count, side, flipped):
    lists = []
    for d in range(depth_count):
        by_row = (d % 2 == 0) != flipped
        for a in range(side):
            cells = [a * side + b if by_row else b * side + a for b in range(side)]
            lists.append([d * side * side + cell for cell in cells])
    return lists


def gather_one(value, axis_groups, side):
    spread = jnp.broadcast_to(value[None], (side,) + value.shape)
    return lax.all_to_all(spread, BOTH, 0, 0, axis_index_groups=axis_groups)


def gather_two(value, depth_count, side):
    first = gather_one(value, groups(depth_count, side, False), side)
    return gather_one(first, groups(depth_count, side, True), side)


def mm(a, b):
    return jnp.dot(a, b, preferred_element_type=F32)


def splits(chips):
    top = (chips * 6 + 15) // 16
    mid = (chips - top + 1) // 2
    return [top, mid, chips - top - mid]


def body(inv_diag, couple, arrow, corner, band_offset):
    depth_count = lax.axis_size("depth")
    lat_count = lax.axis_size("lat")
    side = 4
    depth = lax.axis_index("depth")
    lat = lax.axis_index("lat")
    core = depth % 2
    chip = depth // 2
    chips = depth_count // 2
    g_rows = inv_diag[0]
    share, width = g_rows.shape
    offset = band_offset[0]
    rows = lax.broadcasted_iota(jnp.int32, couple.shape[1:], 0)
    cols = lax.broadcasted_iota(jnp.int32, couple.shape[1:], 1) + lat * share
    keep = jnp.abs(cols - rows - offset) <= HALF
    banded_t = jnp.where(keep, couple[0], jnp.zeros_like(couple[0])).T
    panel = mm(corner, arrow[0]).astype(BF16)
    panel_rows = lax.all_to_all(
        panel.reshape(lat_count, share, share), "lat", 0, 0
    )
    pair = jnp.stack([g_rows, banded_t])
    both = gather_two(pair, depth_count, side)
    g_all = both[:, :, 0].reshape(width, width)
    b_all = both[:, :, 1].reshape(width, width)
    step = -lax.dot_general(
        b_all, g_all, (((0,), (0,)), ((), ())), preferred_element_type=F32
    )
    step = step.astype(BF16)
    p4 = panel_rows.reshape(side, side, share, share)
    p4 = jnp.where(core == 0, p4, jnp.swapaxes(p4, 0, 1))
    p_flat = jnp.transpose(p4, (2, 0, 1, 3)).reshape(share, width)
    bias = -mm(p_flat, g_all)
    sent = jnp.concatenate([step, bias.astype(BF16)])
    swap = [(d, d ^ 1) for d in range(depth_count)]
    got = lax.ppermute(sent, "depth", swap)
    step_odd = jnp.where(core == 1, step, got[:width])
    step_even = jnp.where(core == 0, step, got[:width])
    couple_two = mm(step_odd, step_even).astype(BF16)
    bias_other = got[width:].astype(F32)
    zero = jnp.zeros((share, width), F32)
    add_odd = jnp.where(core == 1, bias, zero)
    add_even = jnp.where(core == 1, mm(bias.astype(BF16), step_even) + bias_other, zero)
    sizes = splits(chips)
    tops, bottoms, top = [], [], chips - 1
    for size in sizes:
        tops.append(top)
        bottoms.append(top - size + 1)
        top -= size
    at_top = (chip == tops[0]) | (chip == tops[1]) | (chip == tops[2])
    r = lax.broadcasted_iota(jnp.int32, (share, width), 0) + lat * share
    c = lax.broadcasted_iota(jnp.int32, (share, width), 1)
    start = (r == c) & at_top & (core == 0)
    v_in = jnp.where(start, 1.0, 0.0).astype(BF16)
    v_even = mm(v_in, couple_two) + add_even
    for hop in range(1, max(sizes)):
        pairs = []
        for block_top, size in zip(tops, sizes):
            if hop < size:
                source, target = block_top - hop + 1, block_top - hop
                pairs += [(2 * source + k, 2 * target + k) for k in range(2)]
        v_in = v_in + lax.ppermute(v_even.astype(BF16), "depth", pairs)
        v_even = mm(v_in, couple_two) + add_even
    v_odd = mm(v_in, step_odd) + add_odd
    mine = jnp.where(core == 0, v_even, v_odd)
    other = lax.ppermute(
        jnp.where(core == 0, v_odd, v_even).astype(BF16), "depth", swap
    )
    map_rows = jnp.where(core == 0, mine.astype(BF16), other)
    own_bias = jnp.where(core == 0, other.astype(F32), mine)
    entry = jnp.zeros((share, width), BF16)
    for target in range(bottoms[1], tops[1] + 1):
        entry = entry + lax.ppermute(
            own_bias.astype(BF16), "depth", [(2 * bottoms[0], 2 * target)]
        )
    maps = gather_two(map_rows, depth_count, side)
    maps = jnp.where(core == 0, maps, jnp.swapaxes(maps, 0, 1)).reshape(width, width)
    middle = mm(entry, maps) + own_bias
    last = jnp.zeros((share, width), BF16)
    for target in range(bottoms[2], tops[2] + 1):
        last = last + lax.ppermute(
            middle.astype(BF16), "depth", [(2 * bottoms[1], 2 * target)]
        )
    entry = entry + last
    entry_odd = lax.ppermute(
        entry, "depth", [(2 * k, 2 * k + 1) for k in range(chips)]
    )
    entry = jnp.where(core == 0, entry, entry_odd)
    return (mm(entry, maps) + own_bias)[None]


def solution(mesh):
    placed = (
        P("depth", "lat", None),
        P("depth", None, "lat"),
        P("depth", None, "lat"),
        P(),
        P("depth"),
    )
    return jax.shard_map(
        body, mesh=mesh, in_specs=placed, out_specs=P("depth", "lat", None), check_vma=False
    )
```

```python
import jax
import jax.numpy as jnp
from jax import lax
from jax.sharding import PartitionSpec as P

HALF = 512
BOTH = ("depth", "lat")
F32 = jnp.float32
BF16 = jnp.bfloat16


def groups(depth_count, side, flipped):
    lists = []
    for d in range(depth_count):
        by_row = (d % 2 == 0) != flipped
        for a in range(side):
            cells = [a * side + b if by_row else b * side + a for b in range(side)]
            lists.append([d * side * side + cell for cell in cells])
    return lists


def gather_one(value, axis_groups, side):
    spread = jnp.broadcast_to(value[None], (side,) + value.shape)
    return lax.all_to_all(spread, BOTH, 0, 0, axis_index_groups=axis_groups)


def gather_two(value, depth_count, side):
    first = gather_one(value, groups(depth_count, side, False), side)
    return gather_one(first, groups(depth_count, side, True), side)


def mm(a, b):
    return jnp.dot(a, b, preferred_element_type=F32)


def body(inv_diag, couple, arrow, corner, band_offset):
    depth_count = lax.axis_size("depth")
    lat_count = lax.axis_size("lat")
    side = 4
    depth = lax.axis_index("depth")
    lat = lax.axis_index("lat")
    core = depth % 2
    chips = depth_count // 2
    g_rows = inv_diag[0]
    share, width = g_rows.shape
    offset = band_offset[0]
    rows = lax.broadcasted_iota(jnp.int32, couple.shape[1:], 0)
    cols = lax.broadcasted_iota(jnp.int32, couple.shape[1:], 1) + lat * share
    keep = jnp.abs(cols - rows - offset) <= HALF
    banded_t = jnp.where(keep, couple[0], jnp.zeros_like(couple[0])).T
    panel = mm(corner, arrow[0]).astype(BF16)
    panel_rows = lax.all_to_all(
        panel.reshape(lat_count, share, share), "lat", 0, 0
    )
    pair = jnp.stack([g_rows, banded_t])
    both = gather_two(pair, depth_count, side)
    g_all = both[:, :, 0].reshape(width, width)
    b_all = both[:, :, 1].reshape(width, width)
    step = -lax.dot_general(
        b_all, g_all, (((0,), (0,)), ((), ())), preferred_element_type=F32
    )
    step = step.astype(BF16)
    p4 = panel_rows.reshape(side, side, share, share)
    p4 = jnp.where(core == 0, p4, jnp.swapaxes(p4, 0, 1))
    p_flat = jnp.transpose(p4, (2, 0, 1, 3)).reshape(share, width)
    bias = -mm(p_flat, g_all)
    half = share // 2
    swap = [(d, d ^ 1) for d in range(depth_count)]
    mates = [[d * lat_count + q, (d + 1) * lat_count + q] for d in range(0, depth_count, 2) for q in range(lat_count)]
    two = lax.all_to_all(
        jnp.broadcast_to(step[None], (2,) + step.shape), BOTH, 0, 0, axis_index_groups=mates
    )
    step_even, step_odd = two[0], two[1]
    low = core == 0
    kept = jnp.where(low, bias[:half], bias[half:])
    got = lax.ppermute(jnp.where(low, bias[half:], bias[:half]), "depth", swap)
    bias_even = jnp.where(low, kept, got)
    bias_odd = jnp.where(low, got, kept)
    entry = jnp.zeros((half, width), BF16)
    for hop in range(chips):
        if hop:
            source = chips - hop
            pairs = [(2 * source + k, 2 * source - 2 + k) for k in range(2)]
            entry = entry + lax.ppermute(x_even.astype(BF16), "depth", pairs)
        x_odd = mm(entry, step_odd) + bias_odd
        x_even = mm(x_odd.astype(BF16), step_even) + bias_even
    mine = jnp.where(low, x_even, x_odd)
    other = lax.ppermute(jnp.where(low, x_odd, x_even), "depth", swap)
    return jnp.where(low, jnp.concatenate([mine, other]), jnp.concatenate([other, mine]))[None]


def solution(mesh):
    placed = (
        P("depth", "lat", None),
        P("depth", None, "lat"),
        P("depth", None, "lat"),
        P(),
        P("depth"),
    )
    return jax.shard_map(
        body, mesh=mesh, in_specs=placed, out_specs=P("depth", "lat", None), check_vma=False
    )
```

```python
import jax
import jax.numpy as jnp
from jax import lax
from jax.experimental import pallas as pl
from jax.experimental.pallas import tpu as pltpu
from jax.sharding import PartitionSpec as P

HALF = 512
BOTH = ("depth", "lat")
F32 = jnp.float32
BF16 = jnp.bfloat16


def groups(depth_count, side, flipped):
    lists = []
    for d in range(depth_count):
        by_row = (d % 2 == 0) != flipped
        for a in range(side):
            cells = [a * side + b if by_row else b * side + a for b in range(side)]
            lists.append([d * side * side + cell for cell in cells])
    return lists


def gather_one(value, axis_groups, side):
    spread = jnp.broadcast_to(value[None], (side,) + value.shape)
    return lax.all_to_all(spread, BOTH, 0, 0, axis_index_groups=axis_groups)


def gather_two(value, depth_count, side):
    first = gather_one(value, groups(depth_count, side, False), side)
    return gather_one(first, groups(depth_count, side, True), side)


def mm(a, b):
    return jnp.dot(a, b, preferred_element_type=F32)


def around(base, side):
    return [(base + shift) % side for shift in (0, -1, 1, 2)]


def ring_moves(depths, side, flipped, shift):
    pairs = []
    for d in depths:
        by_x = (d % 2 == 0) != flipped
        for y in range(side):
            for x in range(side):
                ty, tx = (y, (x + shift) % side) if by_x else ((y + shift) % side, x)
                pairs.append(((d * side + y) * side + x, (d * side + ty) * side + tx))
    return pairs


def ring_gather(value, depths, side, flipped):
    return [value] + [
        lax.ppermute(value, BOTH, ring_moves(depths, side, flipped, shift))
        for shift in (1, -1, 2)
    ]


def sent_down(value, chip_pairs):
    return lax.ppermute(value, "depth", [(2 * a + 1, 2 * b + 1) for a, b in chip_pairs])


def place_kernel(order, a, b, c, d, out):
    count = out.shape[0] // 16
    for g, block in enumerate((a, b, c, d)):
        for f in range(4):
            start = pl.multiple_of(order[4 * g + f] * count, count)
            out[pl.ds(start, count), :] = block[f * count : (f + 1) * count, :]


def place(order, blocks):
    rows, width = blocks[0].shape
    return pl.pallas_call(
        place_kernel,
        out_shape=jax.ShapeDtypeStruct((4 * rows, width), blocks[0].dtype),
        in_specs=[pl.BlockSpec(memory_space=pltpu.SMEM)]
        + [pl.BlockSpec(memory_space=pltpu.VMEM)] * 4,
        out_specs=pl.BlockSpec(memory_space=pltpu.VMEM),
        compiler_params=pltpu.CompilerParams(vmem_limit_bytes=16 * 1024 * 1024),
    )(order, *blocks)


def body(inv_diag, couple, arrow, corner, band_offset):
    depth_count = lax.axis_size("depth")
    lat_count = lax.axis_size("lat")
    side = 4
    depth = lax.axis_index("depth")
    lat = lax.axis_index("lat")
    core = depth % 2
    chip = depth // 2
    chips = depth_count // 2
    g_rows = inv_diag[0]
    share, width = g_rows.shape
    offset = band_offset[0]
    rows = lax.broadcasted_iota(jnp.int32, couple.shape[1:], 0)
    cols = lax.broadcasted_iota(jnp.int32, couple.shape[1:], 1) + lat * share
    keep = jnp.abs(cols - rows - offset) <= HALF
    banded_t = jnp.where(keep, couple[0], jnp.zeros_like(couple[0])).T
    panel = mm(corner, arrow[0]).astype(BF16)
    pair = jnp.stack([g_rows, banded_t])
    both = gather_two(pair, depth_count, side)
    panel, both = lax.optimization_barrier((panel, both))
    panel_rows = lax.all_to_all(
        panel.reshape(lat_count, share, share), "lat", 0, 0
    )
    g_all = both[:, :, 0].reshape(width, width)
    b_all = both[:, :, 1].reshape(width, width)
    step = -lax.dot_general(
        b_all, g_all, (((0,), (0,)), ((), ())), preferred_element_type=F32
    )
    step = step.astype(BF16)
    p4 = panel_rows.reshape(side, side, share, share)
    p4 = jnp.where(core == 0, p4, jnp.swapaxes(p4, 0, 1))
    p_flat = jnp.transpose(p4, (2, 0, 1, 3)).reshape(share, width)
    bias = -mm(p_flat, g_all)
    low = core == 0
    swap = [(d, d ^ 1) for d in range(depth_count)]
    up = [(2 * k, 2 * k + 1) for k in range(chips)]
    got = lax.ppermute(step, "depth", swap)
    step_odd = jnp.where(low, got, step)
    step_even = jnp.where(low, step, got)
    product = mm(step_odd, step_even).astype(BF16)
    bias_other = lax.ppermute(bias, "depth", up)
    zero = jnp.zeros((share, width), F32)
    add_odd = jnp.where(low, zero, bias)
    add_even = jnp.where(low, zero, mm(bias.astype(BF16), got) + bias_other)
    lower = (chips * 6) // 16
    tops = [chips - 1, lower - 1]
    sizes = [chips - lower, lower]
    row = lax.broadcasted_iota(jnp.int32, (share, width), 0) + lat * share
    col = lax.broadcasted_iota(jnp.int32, (share, width), 1)
    start = (row == col) & ((chip == tops[0]) | (chip == tops[1])) & low
    v_in = jnp.where(start, 1.0, 0.0).astype(BF16)
    v_even = mm(v_in, product) + add_even
    for hop in range(1, max(sizes)):
        pairs = []
        for block_top, size in zip(tops, sizes):
            if hop < size:
                source = block_top - hop + 1
                pairs += [(2 * source + k, 2 * source - 2 + k) for k in range(2)]
        v_in = v_in + lax.ppermute(v_even.astype(BF16), "depth", pairs)
        v_even = mm(v_in, product) + add_even
    v_odd = jnp.where(low, mm(v_in, got), mm(v_in, step)) + add_odd
    mine = jnp.where(low, v_even, v_odd)
    other = lax.ppermute(jnp.where(low, v_odd, v_even).astype(BF16), "depth", swap)
    map_rows = jnp.where(low, mine.astype(BF16), other)
    own_bias = jnp.where(low, other.astype(F32), mine)
    depths = range(2 * lower)
    ring = jnp.concatenate(ring_gather(map_rows, depths, side, False))
    edge = v_even.astype(BF16)
    near, far = lower - 1, lower // 2 - 1
    entry = sent_down(edge, [(lower, near)]) + sent_down(edge, [(lower, far)])
    relayed = sent_down(entry, [(near, near - 1), (far, far - 1)])
    last = [(source, source - 2) for source, low_end in ((near, far), (far, -1)) if source - 2 > low_end]
    entry = entry + relayed + sent_down(entry, last)
    y, x = lat // side, lat % side
    order = jnp.stack(
        [
            jnp.where(low, side * b + a, side * a + b)
            for b in around(jnp.where(low, y, x), side)
            for a in around(jnp.where(low, x, y), side)
        ]
    )
    maps = place(order, ring_gather(ring, depths, side, True))
    entry_even = lax.ppermute(
        entry, "depth", [(2 * k + 1, 2 * k) for k in range(lower)]
    )
    entry = jnp.where(low, entry_even, entry)
    return (mm(entry, maps) + own_bias)[None]


def solution(mesh):
    placed = (
        P("depth", "lat", None),
        P("depth", None, "lat"),
        P("depth", None, "lat"),
        P(),
        P("depth"),
    )
    return jax.shard_map(
        body, mesh=mesh, in_specs=placed, out_specs=P("depth", "lat", None), check_vma=False
    )
```

```python
import jax
import jax.numpy as jnp
from jax import lax
from jax.experimental import pallas as pl
from jax.experimental.pallas import tpu as pltpu
from jax.sharding import PartitionSpec as P

HALF = 512
BOTH = ("depth", "lat")
F32 = jnp.float32
BF16 = jnp.bfloat16
SIDE = 4
VMEM = pl.BlockSpec(memory_space=pltpu.VMEM)
SMEM = pl.BlockSpec(memory_space=pltpu.SMEM)
PARAMS = pltpu.CompilerParams(vmem_limit_bytes=32 * 1024 * 1024)


def mm(a, b):
    return jnp.dot(a, b, preferred_element_type=F32)


def around(base):
    return [(base + shift) % SIDE for shift in (0, -1, 1, 2)]


def ring_moves(depths, flipped, shift):
    pairs = []
    for d in depths:
        by_x = (d % 2 == 0) != flipped
        for y in range(SIDE):
            for x in range(SIDE):
                ty, tx = (y, (x + shift) % SIDE) if by_x else ((y + shift) % SIDE, x)
                pairs.append(((d * SIDE + y) * SIDE + x, (d * SIDE + ty) * SIDE + tx))
    return pairs


def ring_gather(value, depths, flipped):
    return [value] + [
        lax.ppermute(value, BOTH, ring_moves(depths, flipped, shift))
        for shift in (1, -1, 2)
    ]


def sent_down(value, chip_pairs):
    return lax.ppermute(value, "depth", [(2 * a + 1, 2 * b + 1) for a, b in chip_pairs])


def place_kernel(order, a, b, c, d, out):
    count = out.shape[0] // 16
    for g, block in enumerate((a, b, c, d)):
        for f in range(4):
            start = pl.multiple_of(order[4 * g + f] * count, count)
            out[pl.ds(start, count), :] = block[f * count : (f + 1) * count, :]


def place(order, blocks):
    rows, width = blocks[0].shape
    return pl.pallas_call(
        place_kernel,
        out_shape=jax.ShapeDtypeStruct((4 * rows, width), blocks[0].dtype),
        in_specs=[SMEM] + [VMEM] * 4,
        out_specs=VMEM,
        compiler_params=PARAMS,
    )(order, *blocks)


def pack_kernel(a, b, c, d, out):
    count = a.shape[1]
    wide = out.shape[1]
    for f, block in enumerate((a, b, c, d)):
        out[0, f * count : (f + 1) * count, :] = block[0]
    for m in range(a.shape[2] // wide):
        cut = slice(m * wide, (m + 1) * wide)
        turned = jnp.concatenate([block[1, :, cut] for block in (a, b, c, d)])
        out[1, :, cut] = turned.T


def pack(blocks):
    two, count, width = blocks[0].shape
    return pl.pallas_call(
        pack_kernel,
        out_shape=jax.ShapeDtypeStruct((two, 4 * count, width), BF16),
        in_specs=[VMEM] * 4,
        out_specs=VMEM,
        compiler_params=PARAMS,
    )(*blocks)


def step_kernel(panel, a, b, c, d, step, bias):
    wide = a.shape[1]
    right = jnp.concatenate([block[0] for block in (a, b, c, d)])
    for m in range(step.shape[0] // wide):
        cut = slice(m * wide, (m + 1) * wide)
        left = jnp.concatenate([block[1, :, cut] for block in (a, b, c, d)], axis=1)
        step[cut, :] = (-mm(left, right)).astype(BF16)
    bias[...] = -mm(panel[...], right)


def step_terms(panel, blocks):
    width = blocks[0].shape[2]
    return pl.pallas_call(
        step_kernel,
        out_shape=[
            jax.ShapeDtypeStruct((width, width), BF16),
            jax.ShapeDtypeStruct(panel.shape, F32),
        ],
        in_specs=[VMEM] * 5,
        out_specs=[VMEM, VMEM],
        compiler_params=PARAMS,
        cost_estimate=pl.CostEstimate(flops=2 * width**3, bytes_accessed=6 * width**2, transcendentals=0),
    )(panel, *blocks)


def product_kernel(core, own, got, bias, bias_got, product, odd, add_even):
    cut = 256
    width = own.shape[0]

    def fill(first, second):
        for m in range(width // cut):
            rows = slice(m * cut, (m + 1) * cut)
            product[rows, :] = mm(first[rows, :], second[...]).astype(BF16)
        odd[...] = first[...]

    @pl.when(core[0] == 0)
    def _():
        fill(got, own)
        add_even[...] = jnp.zeros_like(add_even)

    @pl.when(core[0] != 0)
    def _():
        fill(own, got)
        add_even[...] = mm(bias[...].astype(BF16), got[...]) + bias_got[...]


def products(core, own, got, bias, bias_got):
    width = own.shape[0]
    return pl.pallas_call(
        product_kernel,
        out_shape=[
            jax.ShapeDtypeStruct(own.shape, BF16),
            jax.ShapeDtypeStruct(own.shape, BF16),
            jax.ShapeDtypeStruct(bias.shape, F32),
        ],
        in_specs=[SMEM] + [VMEM] * 4,
        out_specs=[VMEM] * 3,
        compiler_params=PARAMS,
        cost_estimate=pl.CostEstimate(flops=2 * width**3, bytes_accessed=6 * width**2, transcendentals=0),
    )(core.reshape(1), own, got, bias, bias_got)


def body(inv_diag, couple, arrow, corner, band_offset):
    depth_count = lax.axis_size("depth")
    lat_count = lax.axis_size("lat")
    depth = lax.axis_index("depth")
    lat = lax.axis_index("lat")
    core = depth % 2
    chip = depth // 2
    chips = depth_count // 2
    low = core == 0
    y, x = lat // SIDE, lat % SIDE
    order = [
        jnp.where(low, SIDE * b + a, SIDE * a + b)
        for b in around(jnp.where(low, y, x))
        for a in around(jnp.where(low, x, y))
    ]
    g_rows = inv_diag[0]
    share, width = g_rows.shape
    cells = couple[0].T
    row = lax.broadcasted_iota(jnp.int32, cells.shape, 0) + lat * share
    col = lax.broadcasted_iota(jnp.int32, cells.shape, 1)
    keep = jnp.abs(row - col - band_offset[0]) <= HALF
    pair = jnp.stack([g_rows, jnp.where(keep, cells, jnp.zeros_like(cells))])
    panel = mm(corner, arrow[0]).astype(BF16)
    panel_rows = lax.all_to_all(panel.reshape(lat_count, share, share), "lat", 0, 0)
    everyone = range(depth_count)
    first = pack(ring_gather(pair, everyone, False))
    blocks = ring_gather(first, everyone, True)
    panel_cut = jnp.concatenate(
        [lax.dynamic_index_in_dim(panel_rows, q, 0, False) for q in order], axis=1
    )
    step, bias = step_terms(panel_cut, blocks)
    swap = [(d, d ^ 1) for d in range(depth_count)]
    got = lax.ppermute(step, "depth", swap)
    bias_got = lax.ppermute(bias, "depth", [(2 * k, 2 * k + 1) for k in range(chips)])
    product, step_odd, add_even = products(core, step, got, bias, bias_got)
    add_odd = jnp.where(low, jnp.zeros_like(bias), bias)
    lower = (chips * 6) // 16
    tops = [chips - 1, lower - 1]
    sizes = [chips - lower, lower]
    start = (row == col) & ((chip == tops[0]) | (chip == tops[1])) & low
    v_in = jnp.where(start, 1.0, 0.0).astype(BF16)
    v_even = mm(v_in, product) + add_even
    for hop in range(1, max(sizes)):
        pairs = []
        for block_top, size in zip(tops, sizes):
            if hop < size:
                source = block_top - hop + 1
                pairs += [(2 * source + k, 2 * source - 2 + k) for k in range(2)]
        v_in = v_in + lax.ppermute(v_even.astype(BF16), "depth", pairs)
        v_even = mm(v_in, product) + add_even
    edge = v_even.astype(BF16)
    v_odd = mm(v_in, step_odd) + add_odd
    other = lax.ppermute(
        jnp.where(low, v_odd.astype(BF16), edge), "depth", swap[: 2 * lower]
    )
    map_rows = jnp.where(low, edge, other)
    depths = range(2 * lower)
    ring = jnp.concatenate(ring_gather(map_rows, depths, False))
    near, far = lower - 1, lower // 2 - 1
    entry = sent_down(edge, [(lower, near)]) + sent_down(edge, [(lower, far)])
    relayed = sent_down(entry, [(near, near - 1), (far, far - 1)])
    last = [(source, source - 2) for source, low_end in ((near, far), (far, -1)) if source - 2 > low_end]
    entry = entry + relayed + sent_down(entry, last)
    maps = place(jnp.stack(order), ring_gather(ring, depths, True))
    below = chip < lower
    across = lax.ppermute(
        jnp.where(below, entry, edge), "depth", [(2 * k + 1, 2 * k) for k in range(chips)]
    )
    zero = jnp.zeros_like(entry)
    enter = jnp.where(below, jnp.where(low, across, entry), zero)
    own = jnp.where(low, jnp.where(below, other, across).astype(F32), v_odd)
    return (mm(enter, maps) + own)[None]


def solution(mesh):
    placed = (
        P("depth", "lat", None),
        P("depth", None, "lat"),
        P("depth", None, "lat"),
        P(),
        P("depth"),
    )
    return jax.shard_map(
        body, mesh=mesh, in_specs=placed, out_specs=P("depth", "lat", None), check_vma=False
    )
```

```python
import jax
import jax.numpy as jnp
from jax import lax
from jax.experimental import pallas as pl
from jax.experimental.pallas import tpu as pltpu
from jax.sharding import PartitionSpec as P

HALF = 512
BOTH = ("depth", "lat")
F32 = jnp.float32
BF16 = jnp.bfloat16
SIDE = 4
VMEM = pl.BlockSpec(memory_space=pltpu.VMEM)
SMEM = pl.BlockSpec(memory_space=pltpu.SMEM)
PARAMS = pltpu.CompilerParams(vmem_limit_bytes=32 * 1024 * 1024)


def mm(a, b):
    return jnp.dot(a, b, preferred_element_type=F32)


def around(base):
    return [(base + shift) % SIDE for shift in (0, -1, 1, 2)]


def ring_moves(depths, flipped, shift):
    pairs = []
    for d in depths:
        by_x = (d % 2 == 0) != flipped
        for y in range(SIDE):
            for x in range(SIDE):
                ty, tx = (y, (x + shift) % SIDE) if by_x else ((y + shift) % SIDE, x)
                pairs.append(((d * SIDE + y) * SIDE + x, (d * SIDE + ty) * SIDE + tx))
    return pairs


def ring_gather(value, depths, flipped):
    return [value] + [
        lax.ppermute(value, BOTH, ring_moves(depths, flipped, shift))
        for shift in (1, -1, 2)
    ]


def sent_down(value, chip_pairs):
    return lax.ppermute(value, "depth", [(2 * a + 1, 2 * b + 1) for a, b in chip_pairs])


def place_kernel(order, a, b, c, d, out):
    count = out.shape[0] // 16
    for g, block in enumerate((a, b, c, d)):
        for f in range(4):
            start = pl.multiple_of(order[4 * g + f] * count, count)
            out[pl.ds(start, count), :] = block[f * count : (f + 1) * count, :]


def place(order, blocks):
    rows, width = blocks[0].shape
    return pl.pallas_call(
        place_kernel,
        out_shape=jax.ShapeDtypeStruct((4 * rows, width), blocks[0].dtype),
        in_specs=[SMEM] + [VMEM] * 4,
        out_specs=VMEM,
        compiler_params=PARAMS,
    )(order, *blocks)


def pack_kernel(a, b, c, d, out):
    count = a.shape[1]
    wide = out.shape[1]
    for f, block in enumerate((a, b, c, d)):
        out[0, f * count : (f + 1) * count, :] = block[0]
    for m in range(a.shape[2] // wide):
        cut = slice(m * wide, (m + 1) * wide)
        turned = jnp.concatenate([block[1, :, cut] for block in (a, b, c, d)])
        out[1, :, cut] = turned.T


def pack(blocks):
    two, count, width = blocks[0].shape
    return pl.pallas_call(
        pack_kernel,
        out_shape=jax.ShapeDtypeStruct((two, 4 * count, width), BF16),
        in_specs=[VMEM] * 4,
        out_specs=VMEM,
        compiler_params=PARAMS,
    )(*blocks)


def step_kernel(panel, a, b, c, d, step, bias):
    wide = a.shape[1]
    right = jnp.concatenate([block[0] for block in (a, b, c, d)])
    for m in range(step.shape[0] // wide):
        cut = slice(m * wide, (m + 1) * wide)
        left = jnp.concatenate([block[1, :, cut] for block in (a, b, c, d)], axis=1)
        step[cut, :] = (-mm(left, right)).astype(BF16)
    bias[...] = -mm(panel[...], right)


def step_terms(panel, blocks):
    width = blocks[0].shape[2]
    return pl.pallas_call(
        step_kernel,
        out_shape=[
            jax.ShapeDtypeStruct((width, width), BF16),
            jax.ShapeDtypeStruct(panel.shape, F32),
        ],
        in_specs=[VMEM] * 5,
        out_specs=[VMEM, VMEM],
        compiler_params=PARAMS,
        cost_estimate=pl.CostEstimate(flops=2 * width**3, bytes_accessed=6 * width**2, transcendentals=0),
    )(panel, *blocks)


def product_kernel(core, own, got, bias, bias_got, product, odd, add_even):
    cut = 256
    width = own.shape[0]

    def fill(first, second):
        for m in range(width // cut):
            rows = slice(m * cut, (m + 1) * cut)
            product[rows, :] = mm(first[rows, :], second[...]).astype(BF16)
        odd[...] = first[...]

    @pl.when(core[0] == 0)
    def _():
        fill(got, own)
        add_even[...] = jnp.zeros_like(add_even)

    @pl.when(core[0] != 0)
    def _():
        fill(own, got)
        add_even[...] = mm(bias[...].astype(BF16), got[...]) + bias_got[...]


def products(core, own, got, bias, bias_got):
    width = own.shape[0]
    return pl.pallas_call(
        product_kernel,
        out_shape=[
            jax.ShapeDtypeStruct(own.shape, BF16),
            jax.ShapeDtypeStruct(own.shape, BF16),
            jax.ShapeDtypeStruct(bias.shape, F32),
        ],
        in_specs=[SMEM] + [VMEM] * 4,
        out_specs=[VMEM] * 3,
        compiler_params=PARAMS,
        cost_estimate=pl.CostEstimate(flops=2 * width**3, bytes_accessed=6 * width**2, transcendentals=0),
    )(core.reshape(1), own, got, bias, bias_got)


def join_kernel(a, b, ready, out):
    out[...] = a[...] + b[...]


def joined(a, b, ready):
    return pl.pallas_call(
        join_kernel,
        out_shape=jax.ShapeDtypeStruct(a.shape, a.dtype),
        in_specs=[VMEM, VMEM, pl.BlockSpec(memory_space=pl.ANY)],
        out_specs=VMEM,
    )(a, b, ready)


def body(inv_diag, couple, arrow, corner, band_offset):
    depth_count = lax.axis_size("depth")
    lat_count = lax.axis_size("lat")
    depth = lax.axis_index("depth")
    lat = lax.axis_index("lat")
    core = depth % 2
    chip = depth // 2
    chips = depth_count // 2
    low = core == 0
    y, x = lat // SIDE, lat % SIDE
    order = [
        jnp.where(low, SIDE * b + a, SIDE * a + b)
        for b in around(jnp.where(low, y, x))
        for a in around(jnp.where(low, x, y))
    ]
    g_rows = inv_diag[0]
    share, width = g_rows.shape
    cells = couple[0].T
    row = lax.broadcasted_iota(jnp.int32, cells.shape, 0) + lat * share
    col = lax.broadcasted_iota(jnp.int32, cells.shape, 1)
    keep = jnp.abs(row - col - band_offset[0]) <= HALF
    pair = jnp.stack([g_rows, jnp.where(keep, cells, jnp.zeros_like(cells))])
    panel = mm(corner, arrow[0]).astype(BF16)
    panel_rows = lax.all_to_all(panel.reshape(lat_count, share, share), "lat", 0, 0)
    everyone = range(depth_count)
    first = pack(ring_gather(pair, everyone, False))
    blocks = ring_gather(first, everyone, True)
    panel_cut = jnp.concatenate(
        [lax.dynamic_index_in_dim(panel_rows, q, 0, False) for q in order], axis=1
    )
    step, bias = step_terms(panel_cut, blocks)
    swap = [(d, d ^ 1) for d in range(depth_count)]
    got = lax.ppermute(step, "depth", swap)
    bias_got = lax.ppermute(bias, "depth", [(2 * k, 2 * k + 1) for k in range(chips)])
    product, step_odd, add_even = products(core, step, got, bias, bias_got)
    add_odd = jnp.where(low, jnp.zeros_like(bias), bias)
    lower = (chips * 6) // 16
    tops = [chips - 1, lower - 1]
    sizes = [chips - lower, lower]
    start = (row == col) & ((chip == tops[0]) | (chip == tops[1])) & low
    v_in = jnp.where(start, 1.0, 0.0).astype(BF16)
    v_even = mm(v_in, product) + add_even
    for hop in range(1, max(sizes)):
        pairs = []
        for block_top, size in zip(tops, sizes):
            if hop < size:
                source = block_top - hop + 1
                pairs += [(2 * source + k, 2 * source - 2 + k) for k in range(2)]
        v_in = v_in + lax.ppermute(v_even.astype(BF16), "depth", pairs)
        v_even = mm(v_in, product) + add_even
    edge = v_even.astype(BF16)
    v_odd = mm(v_in, step_odd) + add_odd
    other = lax.ppermute(
        jnp.where(low, v_odd.astype(BF16), edge), "depth", swap[: 2 * lower]
    )
    map_rows = jnp.where(low, edge, other)
    depths = range(2 * lower)
    ring = jnp.concatenate(ring_gather(map_rows, depths, False))
    near, far = lower - 1, lower // 2 - 1
    entry = joined(sent_down(edge, [(lower, near)]), sent_down(edge, [(lower, far)]), ring)
    relayed = sent_down(entry, [(near, near - 1), (far, far - 1)])
    last = [(source, source - 2) for source, low_end in ((near, far), (far, -1)) if source - 2 > low_end]
    entry = entry + relayed + sent_down(entry, last)
    maps = place(jnp.stack(order), ring_gather(ring, depths, True))
    below = chip < lower
    across = lax.ppermute(
        jnp.where(below, entry, edge), "depth", [(2 * k + 1, 2 * k) for k in range(chips)]
    )
    zero = jnp.zeros_like(entry)
    enter = jnp.where(below, jnp.where(low, across, entry), zero)
    own = jnp.where(low, jnp.where(below, other, across).astype(F32), v_odd)
    return (mm(enter, maps) + own)[None]


def solution(mesh):
    placed = (
        P("depth", "lat", None),
        P("depth", None, "lat"),
        P("depth", None, "lat"),
        P(),
        P("depth"),
    )
    return jax.shard_map(
        body, mesh=mesh, in_specs=placed, out_specs=P("depth", "lat", None), check_vma=False
    )
```

```python
import jax
import jax.numpy as jnp
from jax import lax
from jax.experimental import pallas as pl
from jax.experimental.pallas import tpu as pltpu
from jax.sharding import PartitionSpec as P

HALF = 512
BOTH = ("depth", "lat")
F32 = jnp.float32
BF16 = jnp.bfloat16
SIDE = 4
VMEM = pl.BlockSpec(memory_space=pltpu.VMEM)
SMEM = pl.BlockSpec(memory_space=pltpu.SMEM)
MIB = 1024 * 1024
PARAMS = pltpu.CompilerParams(vmem_limit_bytes=16 * MIB)
SMALL = pltpu.CompilerParams(vmem_limit_bytes=4 * MIB)


def mm(a, b):
    return jnp.dot(a, b, preferred_element_type=F32)


def around(base):
    return [(base + shift) % SIDE for shift in (0, -1, 1, 2)]


def ring_moves(depths, flipped, shift):
    pairs = []
    for d in depths:
        by_x = (d % 2 == 0) != flipped
        for y in range(SIDE):
            for x in range(SIDE):
                ty, tx = (y, (x + shift) % SIDE) if by_x else ((y + shift) % SIDE, x)
                pairs.append(((d * SIDE + y) * SIDE + x, (d * SIDE + ty) * SIDE + tx))
    return pairs


def ring_gather(value, depths, flipped):
    return [value] + [
        lax.ppermute(value, BOTH, ring_moves(depths, flipped, shift))
        for shift in (1, -1, 2)
    ]


def sent_down(value, chip_pairs):
    return lax.ppermute(value, "depth", [(2 * a + 1, 2 * b + 1) for a, b in chip_pairs])


def place_kernel(order, a, b, c, d, out):
    count = out.shape[0] // 16
    for g, block in enumerate((a, b, c, d)):
        for f in range(4):
            start = pl.multiple_of(order[4 * g + f] * count, count)
            out[pl.ds(start, count), :] = block[f * count : (f + 1) * count, :]


def place(order, blocks):
    rows, width = blocks[0].shape
    return pl.pallas_call(
        place_kernel,
        out_shape=jax.ShapeDtypeStruct((4 * rows, width), blocks[0].dtype),
        in_specs=[SMEM] + [VMEM] * 4,
        out_specs=VMEM,
        compiler_params=PARAMS,
    )(order, *blocks)


def pack_kernel(a, b, c, d, out):
    count = a.shape[1]
    wide = out.shape[1]
    for f, block in enumerate((a, b, c, d)):
        out[0, f * count : (f + 1) * count, :] = block[0]
    for m in range(a.shape[2] // wide):
        cut = slice(m * wide, (m + 1) * wide)
        turned = jnp.concatenate([block[1, :, cut] for block in (a, b, c, d)])
        out[1, :, cut] = turned.T


def pack(blocks):
    two, count, width = blocks[0].shape
    return pl.pallas_call(
        pack_kernel,
        out_shape=jax.ShapeDtypeStruct((two, 4 * count, width), BF16),
        in_specs=[VMEM] * 4,
        out_specs=VMEM,
        compiler_params=PARAMS,
    )(*blocks)


def step_kernel(panel, a, b, c, d, step, bias):
    wide = a.shape[1]
    right = jnp.concatenate([block[0] for block in (a, b, c, d)])
    for m in range(step.shape[0] // wide):
        cut = slice(m * wide, (m + 1) * wide)
        left = jnp.concatenate([block[1, :, cut] for block in (a, b, c, d)], axis=1)
        step[cut, :] = (-mm(left, right)).astype(BF16)
    bias[...] = -mm(panel[...], right)


def step_terms(panel, blocks):
    width = blocks[0].shape[2]
    return pl.pallas_call(
        step_kernel,
        out_shape=[
            jax.ShapeDtypeStruct((width, width), BF16),
            jax.ShapeDtypeStruct(panel.shape, F32),
        ],
        in_specs=[VMEM] * 5,
        out_specs=[VMEM, VMEM],
        compiler_params=PARAMS,
        cost_estimate=pl.CostEstimate(flops=2 * width**3, bytes_accessed=6 * width**2, transcendentals=0),
    )(panel, *blocks)


def product_kernel(core, own, got, bias, bias_got, product, odd, add_even):
    cut = 256
    width = own.shape[0]

    def fill(first, second):
        for m in range(width // cut):
            rows = slice(m * cut, (m + 1) * cut)
            product[rows, :] = mm(first[rows, :], second[...]).astype(BF16)
        odd[...] = first[...]

    @pl.when(core[0] == 0)
    def _():
        fill(got, own)
        add_even[...] = jnp.zeros_like(add_even)

    @pl.when(core[0] != 0)
    def _():
        fill(own, got)
        add_even[...] = mm(bias[...].astype(BF16), got[...]) + bias_got[...]


def products(core, own, got, bias, bias_got):
    width = own.shape[0]
    return pl.pallas_call(
        product_kernel,
        out_shape=[
            jax.ShapeDtypeStruct(own.shape, BF16),
            jax.ShapeDtypeStruct(own.shape, BF16),
            jax.ShapeDtypeStruct(bias.shape, F32),
        ],
        in_specs=[SMEM] + [VMEM] * 4,
        out_specs=[VMEM] * 3,
        compiler_params=PARAMS,
        cost_estimate=pl.CostEstimate(flops=2 * width**3, bytes_accessed=6 * width**2, transcendentals=0),
    )(core.reshape(1), own, got, bias, bias_got)


def join_kernel(a, b, ready, out):
    out[...] = a[...] + b[...]


def joined(a, b, ready):
    return pl.pallas_call(
        join_kernel,
        out_shape=jax.ShapeDtypeStruct(a.shape, a.dtype),
        in_specs=[VMEM, VMEM, VMEM],
        out_specs=VMEM,
        compiler_params=SMALL,
    )(a, b, ready)


def settle_kernel(flags, entry, relayed, last, edge, out):
    @pl.when(flags[1] != 0)
    def _():
        out[...] = entry[...] + relayed[...] + last[...]

    @pl.when(flags[1] == 0)
    def _():
        out[...] = edge[...]


def settled(flags, entry, relayed, last, edge):
    return pl.pallas_call(
        settle_kernel,
        out_shape=jax.ShapeDtypeStruct(entry.shape, entry.dtype),
        in_specs=[SMEM] + [VMEM] * 4,
        out_specs=VMEM,
        compiler_params=SMALL,
    )(flags, entry, relayed, last, edge)


def close_kernel(flags, maps, entry, across, other, v_odd, out):
    low, below = flags[0] != 0, flags[1] != 0

    @pl.when(low & below)
    def _():
        out[...] = mm(across[...], maps[...]) + other[...].astype(F32)

    @pl.when(low & jnp.logical_not(below))
    def _():
        out[...] = across[...].astype(F32)

    @pl.when(jnp.logical_not(low) & below)
    def _():
        out[...] = mm(entry[...], maps[...]) + v_odd[...]

    @pl.when(jnp.logical_not(low) & jnp.logical_not(below))
    def _():
        out[...] = v_odd[...]


def closed(flags, maps, entry, across, other, v_odd):
    return pl.pallas_call(
        close_kernel,
        out_shape=jax.ShapeDtypeStruct(entry.shape, F32),
        in_specs=[SMEM] + [VMEM] * 5,
        out_specs=VMEM,
        compiler_params=PARAMS,
    )(flags, maps, entry, across, other, v_odd)


def body(inv_diag, couple, arrow, corner, band_offset):
    depth_count = lax.axis_size("depth")
    lat_count = lax.axis_size("lat")
    depth = lax.axis_index("depth")
    lat = lax.axis_index("lat")
    core = depth % 2
    chip = depth // 2
    chips = depth_count // 2
    low = core == 0
    y, x = lat // SIDE, lat % SIDE
    order = [
        jnp.where(low, SIDE * b + a, SIDE * a + b)
        for b in around(jnp.where(low, y, x))
        for a in around(jnp.where(low, x, y))
    ]
    g_rows = inv_diag[0]
    share, width = g_rows.shape
    cells = couple[0].T
    row = lax.broadcasted_iota(jnp.int32, cells.shape, 0) + lat * share
    col = lax.broadcasted_iota(jnp.int32, cells.shape, 1)
    keep = jnp.abs(row - col - band_offset[0]) <= HALF
    pair = jnp.stack([g_rows, jnp.where(keep, cells, jnp.zeros_like(cells))])
    panel = mm(corner, arrow[0]).astype(BF16)
    panel_rows = lax.all_to_all(panel.reshape(lat_count, share, share), "lat", 0, 0)
    everyone = range(depth_count)
    first = pack(ring_gather(pair, everyone, False))
    blocks = ring_gather(first, everyone, True)
    panel_cut = jnp.concatenate(
        [lax.dynamic_index_in_dim(panel_rows, q, 0, False) for q in order], axis=1
    )
    step, bias = step_terms(panel_cut, blocks)
    swap = [(d, d ^ 1) for d in range(depth_count)]
    got = lax.ppermute(step, "depth", swap)
    bias_got = lax.ppermute(bias, "depth", [(2 * k, 2 * k + 1) for k in range(chips)])
    product, step_odd, add_even = products(core, step, got, bias, bias_got)
    add_odd = jnp.where(low, jnp.zeros_like(bias), bias)
    lower = (chips * 5) // 16
    tops = [chips - 1, lower - 1]
    sizes = [chips - lower, lower]
    start = (row == col) & ((chip == tops[0]) | (chip == tops[1])) & low
    v_in = jnp.where(start, 1.0, 0.0).astype(BF16)
    v_even = mm(v_in, product) + add_even
    for hop in range(1, max(sizes)):
        pairs = []
        for block_top, size, cores in zip(tops, sizes, ((1,), (0, 1))):
            if hop < size:
                source = block_top - hop + 1
                pairs += [(2 * source + k, 2 * source - 2 + k) for k in cores]
        v_in = v_in + lax.ppermute(v_even.astype(BF16), "depth", pairs)
        v_even = mm(v_in, product) + add_even
    edge = v_even.astype(BF16)
    v_odd = mm(v_in, step_odd) + add_odd
    other = lax.ppermute(
        jnp.where(low, v_odd.astype(BF16), edge), "depth", swap[: 2 * lower]
    )
    map_rows = jnp.where(low, edge, other)
    depths = range(2 * lower)
    ring = jnp.concatenate(ring_gather(map_rows, depths, False))
    near, far = lower - 1, lower // 2 - 1
    entry = joined(sent_down(edge, [(lower, near)]), sent_down(edge, [(lower, far)]), ring)
    relayed = sent_down(entry, [(near, near - 1), (far, far - 1)])
    last = [(source, source - 2) for source, low_end in ((near, far), (far, -1)) if source - 2 > low_end]
    last = sent_down(entry, last)
    maps = place(jnp.stack(order), ring_gather(ring, depths, True))
    below = chip < lower
    flags = jnp.stack([low, below]).astype(jnp.int32)
    entry = settled(flags, entry, relayed, last, edge)
    across = lax.ppermute(entry, "depth", [(2 * k + 1, 2 * k) for k in range(chips)])
    return closed(flags, maps, entry, across, other, v_odd)[None]


def solution(mesh):
    placed = (
        P("depth", "lat", None),
        P("depth", None, "lat"),
        P("depth", None, "lat"),
        P(),
        P("depth"),
    )
    return jax.shard_map(
        body, mesh=mesh, in_specs=placed, out_specs=P("depth", "lat", None), check_vma=False
    )
```

```python
import jax
import jax.numpy as jnp
from jax import lax
from jax.experimental import pallas as pl
from jax.experimental.pallas import tpu as pltpu
from jax.sharding import PartitionSpec as P

HALF = 512
BOTH = ("depth", "lat")
F32 = jnp.float32
BF16 = jnp.bfloat16
SIDE = 4
VMEM = pl.BlockSpec(memory_space=pltpu.VMEM)
SMEM = pl.BlockSpec(memory_space=pltpu.SMEM)
MIB = 1024 * 1024
PARAMS = pltpu.CompilerParams(vmem_limit_bytes=16 * MIB)
SMALL = pltpu.CompilerParams(vmem_limit_bytes=4 * MIB)


def mm(a, b):
    return jnp.dot(a, b, preferred_element_type=F32)


def around(base):
    return [(base + shift) % SIDE for shift in (0, -1, 1, 2)]


def ring_moves(depths, flipped, shift):
    pairs = []
    for d in depths:
        by_x = (d % 2 == 0) != flipped
        for y in range(SIDE):
            for x in range(SIDE):
                ty, tx = (y, (x + shift) % SIDE) if by_x else ((y + shift) % SIDE, x)
                pairs.append(((d * SIDE + y) * SIDE + x, (d * SIDE + ty) * SIDE + tx))
    return pairs


def ring_gather(value, depths, flipped):
    return [value] + [
        lax.ppermute(value, BOTH, ring_moves(depths, flipped, shift))
        for shift in (1, -1, 2)
    ]


def sent_down(value, chip_pairs):
    return lax.ppermute(value, "depth", [(2 * a + 1, 2 * b + 1) for a, b in chip_pairs])


def place_kernel(order, a, b, c, d, out):
    count = out.shape[0] // 16
    for g, block in enumerate((a, b, c, d)):
        for f in range(4):
            start = pl.multiple_of(order[4 * g + f] * count, count)
            out[pl.ds(start, count), :] = block[f * count : (f + 1) * count, :]


def place(order, blocks):
    rows, width = blocks[0].shape
    return pl.pallas_call(
        place_kernel,
        out_shape=jax.ShapeDtypeStruct((4 * rows, width), blocks[0].dtype),
        in_specs=[SMEM] + [VMEM] * 4,
        out_specs=VMEM,
        compiler_params=PARAMS,
    )(order, *blocks)


def pack_kernel(a, b, c, d, out):
    count = a.shape[1]
    wide = out.shape[1]
    for f, block in enumerate((a, b, c, d)):
        out[0, f * count : (f + 1) * count, :] = block[0]
    for m in range(a.shape[2] // wide):
        cut = slice(m * wide, (m + 1) * wide)
        turned = jnp.concatenate([block[1, :, cut] for block in (a, b, c, d)])
        out[1, :, cut] = turned.T


def pack(blocks):
    two, count, width = blocks[0].shape
    return pl.pallas_call(
        pack_kernel,
        out_shape=jax.ShapeDtypeStruct((two, 4 * count, width), BF16),
        in_specs=[VMEM] * 4,
        out_specs=VMEM,
        compiler_params=PARAMS,
    )(*blocks)


def half_product(first, second, cut):
    left = jnp.concatenate([first[1, :, cut], second[1, :, cut]], axis=1)
    return mm(left, jnp.concatenate([first[0], second[0]]))


def part_kernel(a, d, out, token):
    token[...] = jnp.zeros_like(token)
    wide = a.shape[1]
    for m in range(out.shape[0] // wide):
        cut = slice(m * wide, (m + 1) * wide)
        out[cut, :] = half_product(a, d, cut).astype(BF16)


def step_kernel(panel, part, b, c, a_right, d_right, step, bias):
    wide = b.shape[1]
    for m in range(step.shape[0] // wide):
        cut = slice(m * wide, (m + 1) * wide)
        step[cut, :] = (-(part[cut, :].astype(F32) + half_product(b, c, cut))).astype(BF16)
    total = mm(panel[:, :wide], a_right[0])
    for f, right in ((1, b), (2, c), (3, d_right)):
        total = total + mm(panel[:, f * wide : (f + 1) * wide], right[0])
    bias[...] = -total


def cut_kernel(order, panel, ready, out):
    share = panel.shape[2] // 2
    for i in range(0, panel.shape[0], 2):
        two = [panel[order[i]].astype(F32), panel[order[i + 1]].astype(F32)]
        upper = jnp.concatenate([part[:, :share] for part in two], axis=1)
        under = jnp.concatenate([part[:, share:] for part in two], axis=1)
        both = jnp.concatenate([upper, under]).astype(BF16)
        out[:, i * share : (i + 2) * share] = both


def step_terms(order, panel, blocks):
    a, b, c, d = blocks
    two, wide, width = a.shape
    cost = pl.CostEstimate(flops=width**3, bytes_accessed=6 * width**2, transcendentals=0)
    part, token = pl.pallas_call(
        part_kernel,
        out_shape=[
            jax.ShapeDtypeStruct((width, width), BF16),
            jax.ShapeDtypeStruct((8, 128), F32),
        ],
        in_specs=[VMEM] * 2,
        out_specs=[VMEM, VMEM],
        compiler_params=PARAMS,
        cost_estimate=cost,
    )(a, d)
    panel = pl.pallas_call(
        cut_kernel,
        out_shape=jax.ShapeDtypeStruct((2 * panel.shape[1], width), BF16),
        in_specs=[SMEM, VMEM, VMEM],
        out_specs=VMEM,
        compiler_params=SMALL,
    )(order, panel, token)

    def whole(shape):
        return pl.BlockSpec(shape, lambda i: (0,) * len(shape))

    right = whole((1, wide, width))
    return pl.pallas_call(
        step_kernel,
        out_shape=[
            jax.ShapeDtypeStruct((width, width), BF16),
            jax.ShapeDtypeStruct(panel.shape, F32),
        ],
        in_specs=[VMEM, VMEM, VMEM, VMEM, right, right],
        out_specs=[VMEM, VMEM],
        grid=(1,),
        compiler_params=PARAMS,
        cost_estimate=cost,
    )(panel, part, b, c, a, d)


def product_kernel(core, own, got, bias, bias_got, product, odd, add_even):
    cut = 256
    width = own.shape[0]

    def fill(first, second):
        for m in range(width // cut):
            rows = slice(m * cut, (m + 1) * cut)
            product[rows, :] = mm(first[rows, :], second[...]).astype(BF16)
        odd[...] = first[...]

    @pl.when(core[0] == 0)
    def _():
        fill(got, own)
        add_even[...] = jnp.zeros_like(add_even)

    @pl.when(core[0] != 0)
    def _():
        fill(own, got)
        add_even[...] = mm(bias[...].astype(BF16), got[...]) + bias_got[...]


def products(core, own, got, bias, bias_got):
    width = own.shape[0]
    return pl.pallas_call(
        product_kernel,
        out_shape=[
            jax.ShapeDtypeStruct(own.shape, BF16),
            jax.ShapeDtypeStruct(own.shape, BF16),
            jax.ShapeDtypeStruct(bias.shape, F32),
        ],
        in_specs=[SMEM] + [VMEM] * 4,
        out_specs=[VMEM] * 3,
        compiler_params=PARAMS,
        cost_estimate=pl.CostEstimate(flops=2 * width**3, bytes_accessed=6 * width**2, transcendentals=0),
    )(core.reshape(1), own, got, bias, bias_got)


def join_kernel(a, b, ready, out):
    out[...] = a[...] + b[...]


def joined(a, b, ready):
    return pl.pallas_call(
        join_kernel,
        out_shape=jax.ShapeDtypeStruct(a.shape, a.dtype),
        in_specs=[VMEM, VMEM, VMEM],
        out_specs=VMEM,
        compiler_params=SMALL,
    )(a, b, ready)


def settle_kernel(flags, entry, relayed, last, edge, out):
    @pl.when(flags[1] != 0)
    def _():
        out[...] = entry[...] + relayed[...] + last[...]

    @pl.when(flags[1] == 0)
    def _():
        out[...] = edge[...]


def settled(flags, entry, relayed, last, edge):
    return pl.pallas_call(
        settle_kernel,
        out_shape=jax.ShapeDtypeStruct(entry.shape, entry.dtype),
        in_specs=[SMEM] + [VMEM] * 4,
        out_specs=VMEM,
        compiler_params=SMALL,
    )(flags, entry, relayed, last, edge)


def close_kernel(flags, maps, entry, across, other, v_odd, out):
    low, below = flags[0] != 0, flags[1] != 0

    @pl.when(low & below)
    def _():
        out[...] = mm(across[...], maps[...]) + other[...].astype(F32)

    @pl.when(low & jnp.logical_not(below))
    def _():
        out[...] = across[...].astype(F32)

    @pl.when(jnp.logical_not(low) & below)
    def _():
        out[...] = mm(entry[...], maps[...]) + v_odd[...]

    @pl.when(jnp.logical_not(low) & jnp.logical_not(below))
    def _():
        out[...] = v_odd[...]


def closed(flags, maps, entry, across, other, v_odd):
    return pl.pallas_call(
        close_kernel,
        out_shape=jax.ShapeDtypeStruct(entry.shape, F32),
        in_specs=[SMEM] + [VMEM] * 5,
        out_specs=VMEM,
        compiler_params=PARAMS,
    )(flags, maps, entry, across, other, v_odd)


def body(inv_diag, couple, arrow, corner, band_offset):
    depth_count = lax.axis_size("depth")
    lat_count = lax.axis_size("lat")
    depth = lax.axis_index("depth")
    lat = lax.axis_index("lat")
    core = depth % 2
    chip = depth // 2
    chips = depth_count // 2
    low = core == 0
    y, x = lat // SIDE, lat % SIDE
    order = [
        jnp.where(low, SIDE * b + a, SIDE * a + b)
        for b in around(jnp.where(low, y, x))
        for a in around(jnp.where(low, x, y))
    ]
    g_rows = inv_diag[0]
    share, width = g_rows.shape
    cells = couple[0].T
    row = lax.broadcasted_iota(jnp.int32, cells.shape, 0) + lat * share
    col = lax.broadcasted_iota(jnp.int32, cells.shape, 1)
    keep = jnp.abs(row - col - band_offset[0]) <= HALF
    pair = jnp.stack([g_rows, jnp.where(keep, cells, jnp.zeros_like(cells))])
    panel = mm(corner, arrow[0]).astype(BF16).reshape(lat_count, 2, share // 2, share)
    panel = jnp.swapaxes(panel, 1, 2).reshape(lat_count, share // 2, 2 * share)
    panel_rows = lax.all_to_all(panel, "lat", 0, 0)
    everyone = range(depth_count)
    first = pack(ring_gather(pair, everyone, False))
    blocks = ring_gather(first, everyone, True)
    order = jnp.stack(order)
    step, bias = step_terms(order, panel_rows, blocks)
    swap = [(d, d ^ 1) for d in range(depth_count)]
    got = lax.ppermute(step, "depth", swap)
    bias_got = lax.ppermute(bias, "depth", [(2 * k, 2 * k + 1) for k in range(chips)])
    product, step_odd, add_even = products(core, step, got, bias, bias_got)
    add_odd = jnp.where(low, jnp.zeros_like(bias), bias)
    lower = (chips * 6) // 16
    tops = [chips - 1, lower - 1]
    sizes = [chips - lower, lower]
    start = (row == col) & ((chip == tops[0]) | (chip == tops[1])) & low
    v_in = jnp.where(start, 1.0, 0.0).astype(BF16)
    v_even = mm(v_in, product) + add_even
    for hop in range(1, max(sizes)):
        pairs = []
        for block_top, size, cores in zip(tops, sizes, ((1,), (0, 1))):
            if hop < size:
                source = block_top - hop + 1
                pairs += [(2 * source + k, 2 * source - 2 + k) for k in cores]
        v_in = v_in + lax.ppermute(v_even.astype(BF16), "depth", pairs)
        v_even = mm(v_in, product) + add_even
    edge = v_even.astype(BF16)
    v_odd = mm(v_in, step_odd) + add_odd
    other = lax.ppermute(
        jnp.where(low, v_odd.astype(BF16), edge), "depth", swap[: 2 * lower]
    )
    map_rows = jnp.where(low, edge, other)
    depths = range(2 * lower)
    ring = jnp.concatenate(ring_gather(map_rows, depths, False))
    near, far = lower - 1, lower // 2 - 1
    entry = joined(sent_down(edge, [(lower, near)]), sent_down(edge, [(lower, far)]), ring)
    relayed = sent_down(entry, [(near, near - 1), (far, far - 1)])
    last = [(source, source - 2) for source, low_end in ((near, far), (far, -1)) if source - 2 > low_end]
    last = sent_down(entry, last)
    maps = place(order, ring_gather(ring, depths, True))
    below = chip < lower
    flags = jnp.stack([low, below]).astype(jnp.int32)
    entry = settled(flags, entry, relayed, last, edge)
    across = lax.ppermute(entry, "depth", [(2 * k + 1, 2 * k) for k in range(chips)])
    return closed(flags, maps, entry, across, other, v_odd)[None]


def solution(mesh):
    placed = (
        P("depth", "lat", None),
        P("depth", None, "lat"),
        P("depth", None, "lat"),
        P(),
        P("depth"),
    )
    return jax.shard_map(
        body, mesh=mesh, in_specs=placed, out_specs=P("depth", "lat", None), check_vma=False
    )
```

```python
import jax
import jax.numpy as jnp
from jax import lax
from jax.experimental import pallas as pl
from jax.experimental.pallas import tpu as pltpu
from jax.sharding import PartitionSpec as P

HALF = 512
BOTH = ("depth", "lat")
F32 = jnp.float32
BF16 = jnp.bfloat16
SIDE = 4
VMEM = pl.BlockSpec(memory_space=pltpu.VMEM)
SMEM = pl.BlockSpec(memory_space=pltpu.SMEM)
MIB = 1024 * 1024
PARAMS = pltpu.CompilerParams(vmem_limit_bytes=16 * MIB)
SMALL = pltpu.CompilerParams(vmem_limit_bytes=4 * MIB)


def mm(a, b):
    return jnp.dot(a, b, preferred_element_type=F32)


def around(base):
    return [(base + shift) % SIDE for shift in (0, -1, 1, 2)]


def ring_moves(depths, flipped, shift):
    pairs = []
    for d in depths:
        by_x = (d % 2 == 0) != flipped
        for y in range(SIDE):
            for x in range(SIDE):
                ty, tx = (y, (x + shift) % SIDE) if by_x else ((y + shift) % SIDE, x)
                pairs.append(((d * SIDE + y) * SIDE + x, (d * SIDE + ty) * SIDE + tx))
    return pairs


def ring_gather(value, depths, flipped):
    return [value] + [
        lax.ppermute(value, BOTH, ring_moves(depths, flipped, shift))
        for shift in (1, -1, 2)
    ]


def sent_down(value, chip_pairs):
    return lax.ppermute(value, "depth", [(2 * a + 1, 2 * b + 1) for a, b in chip_pairs])


def place_kernel(order, a, b, c, d, out):
    count = out.shape[0] // 16
    for g, block in enumerate((a, b, c, d)):
        for f in range(4):
            start = pl.multiple_of(order[4 * g + f] * count, count)
            out[pl.ds(start, count), :] = block[f * count : (f + 1) * count, :]


def place(order, blocks):
    rows, width = blocks[0].shape
    return pl.pallas_call(
        place_kernel,
        out_shape=jax.ShapeDtypeStruct((4 * rows, width), blocks[0].dtype),
        in_specs=[SMEM] + [VMEM] * 4,
        out_specs=VMEM,
        compiler_params=PARAMS,
    )(order, *blocks)


def pack_kernel(a, b, c, d, out):
    count = a.shape[1]
    wide = out.shape[1]
    for f, block in enumerate((a, b, c, d)):
        out[0, f * count : (f + 1) * count, :] = block[0]
    for m in range(a.shape[2] // wide):
        cut = slice(m * wide, (m + 1) * wide)
        turned = jnp.concatenate([block[1, :, cut] for block in (a, b, c, d)])
        out[1, :, cut] = turned.T


def pack(blocks):
    two, count, width = blocks[0].shape
    return pl.pallas_call(
        pack_kernel,
        out_shape=jax.ShapeDtypeStruct((two, 4 * count, width), BF16),
        in_specs=[VMEM] * 4,
        out_specs=VMEM,
        compiler_params=PARAMS,
    )(*blocks)


def half_product(first, second, cut):
    left = jnp.concatenate([first[1, :, cut], second[1, :, cut]], axis=1)
    return mm(left, jnp.concatenate([first[0], second[0]]))


def part_kernel(a, d, out, token):
    token[...] = jnp.zeros_like(token)
    wide = a.shape[1]
    for m in range(out.shape[0] // wide):
        cut = slice(m * wide, (m + 1) * wide)
        out[cut, :] = half_product(a, d, cut).astype(BF16)


def step_kernel(part, b, c, step, token):
    token[...] = jnp.zeros_like(token)
    wide = b.shape[1]
    for m in range(step.shape[0] // wide):
        cut = slice(m * wide, (m + 1) * wide)
        step[cut, :] = (-(part[cut, :].astype(F32) + half_product(b, c, cut))).astype(BF16)


def bias_kernel(panel, a, b, c, d, bias):
    wide = a.shape[1]
    total = mm(panel[:, :wide], a[0])
    for f, right in ((1, b), (2, c), (3, d)):
        total = total + mm(panel[:, f * wide : (f + 1) * wide], right[0])
    bias[...] = -total


def cut_kernel(order, panel, ready, out):
    share = panel.shape[2] // 2
    for i in range(0, panel.shape[0], 2):
        two = [panel[order[i]].astype(F32), panel[order[i + 1]].astype(F32)]
        upper = jnp.concatenate([part[:, :share] for part in two], axis=1)
        under = jnp.concatenate([part[:, share:] for part in two], axis=1)
        both = jnp.concatenate([upper, under]).astype(BF16)
        out[:, i * share : (i + 2) * share] = both


def step_terms(order, panel, blocks):
    a, b, c, d = blocks
    two, wide, width = a.shape
    whole = jax.ShapeDtypeStruct((width, width), BF16)
    token = jax.ShapeDtypeStruct((8, 128), F32)
    part, unused = pl.pallas_call(
        part_kernel,
        out_shape=[whole, token],
        in_specs=[VMEM] * 2,
        out_specs=[VMEM, VMEM],
        compiler_params=PARAMS,
    )(a, d)
    step, ready = pl.pallas_call(
        step_kernel,
        out_shape=[whole, token],
        in_specs=[VMEM] * 3,
        out_specs=[VMEM, VMEM],
        compiler_params=PARAMS,
    )(part, b, c)
    rows = 2 * panel.shape[1]
    panel = pl.pallas_call(
        cut_kernel,
        out_shape=jax.ShapeDtypeStruct((rows, width), BF16),
        in_specs=[SMEM, VMEM, VMEM],
        out_specs=VMEM,
        compiler_params=SMALL,
    )(order, panel, ready)
    flat = pl.BlockSpec((rows, width), lambda i: (0, 0))
    bias = pl.pallas_call(
        bias_kernel,
        out_shape=jax.ShapeDtypeStruct((rows, width), F32),
        in_specs=[flat] + [pl.BlockSpec((1, wide, width), lambda i: (0, 0, 0))] * 4,
        out_specs=flat,
        grid=(1,),
        compiler_params=PARAMS,
        cost_estimate=pl.CostEstimate(flops=40 * width**3, bytes_accessed=6 * width**2, transcendentals=0),
    )(panel, a, b, c, d)
    return step, bias


def product_kernel(core, own, got, bias, bias_got, product, odd, add_even):
    cut = 256
    width = own.shape[0]

    def fill(first, second):
        for m in range(width // cut):
            rows = slice(m * cut, (m + 1) * cut)
            product[rows, :] = mm(first[rows, :], second[...]).astype(BF16)
        odd[...] = first[...]

    @pl.when(core[0] == 0)
    def _():
        fill(got, own)
        add_even[...] = jnp.zeros_like(add_even)

    @pl.when(core[0] != 0)
    def _():
        fill(own, got)
        add_even[...] = mm(bias[...].astype(BF16), got[...]) + bias_got[...]


def products(core, own, got, bias, bias_got):
    width = own.shape[0]
    return pl.pallas_call(
        product_kernel,
        out_shape=[
            jax.ShapeDtypeStruct(own.shape, BF16),
            jax.ShapeDtypeStruct(own.shape, BF16),
            jax.ShapeDtypeStruct(bias.shape, F32),
        ],
        in_specs=[SMEM] + [VMEM] * 4,
        out_specs=[VMEM] * 3,
        compiler_params=PARAMS,
        cost_estimate=pl.CostEstimate(flops=2 * width**3, bytes_accessed=6 * width**2, transcendentals=0),
    )(core.reshape(1), own, got, bias, bias_got)


def join_kernel(a, b, ready, out):
    out[...] = a[...] + b[...]


def joined(a, b, ready):
    return pl.pallas_call(
        join_kernel,
        out_shape=jax.ShapeDtypeStruct(a.shape, a.dtype),
        in_specs=[VMEM, VMEM, VMEM],
        out_specs=VMEM,
        compiler_params=SMALL,
    )(a, b, ready)


def settle_kernel(flags, entry, relayed, last, edge, out):
    @pl.when(flags[1] != 0)
    def _():
        out[...] = entry[...] + relayed[...] + last[...]

    @pl.when(flags[1] == 0)
    def _():
        out[...] = edge[...]


def settled(flags, entry, relayed, last, edge):
    return pl.pallas_call(
        settle_kernel,
        out_shape=jax.ShapeDtypeStruct(entry.shape, entry.dtype),
        in_specs=[SMEM] + [VMEM] * 4,
        out_specs=VMEM,
        compiler_params=SMALL,
    )(flags, entry, relayed, last, edge)


def close_kernel(flags, maps, entry, across, other, v_odd, out):
    low, below = flags[0] != 0, flags[1] != 0

    @pl.when(low & below)
    def _():
        out[...] = mm(across[...], maps[...]) + other[...].astype(F32)

    @pl.when(low & jnp.logical_not(below))
    def _():
        out[...] = across[...].astype(F32)

    @pl.when(jnp.logical_not(low) & below)
    def _():
        out[...] = mm(entry[...], maps[...]) + v_odd[...]

    @pl.when(jnp.logical_not(low) & jnp.logical_not(below))
    def _():
        out[...] = v_odd[...]


def closed(flags, maps, entry, across, other, v_odd):
    return pl.pallas_call(
        close_kernel,
        out_shape=jax.ShapeDtypeStruct(entry.shape, F32),
        in_specs=[SMEM] + [VMEM] * 5,
        out_specs=VMEM,
        compiler_params=PARAMS,
    )(flags, maps, entry, across, other, v_odd)


def body(inv_diag, couple, arrow, corner, band_offset):
    depth_count = lax.axis_size("depth")
    lat_count = lax.axis_size("lat")
    depth = lax.axis_index("depth")
    lat = lax.axis_index("lat")
    core = depth % 2
    chip = depth // 2
    chips = depth_count // 2
    low = core == 0
    y, x = lat // SIDE, lat % SIDE
    order = [
        jnp.where(low, SIDE * b + a, SIDE * a + b)
        for b in around(jnp.where(low, y, x))
        for a in around(jnp.where(low, x, y))
    ]
    g_rows = inv_diag[0]
    share, width = g_rows.shape
    cells = couple[0].T
    row = lax.broadcasted_iota(jnp.int32, cells.shape, 0) + lat * share
    col = lax.broadcasted_iota(jnp.int32, cells.shape, 1)
    keep = jnp.abs(row - col - band_offset[0]) <= HALF
    pair = jnp.stack([g_rows, jnp.where(keep, cells, jnp.zeros_like(cells))])
    panel = mm(corner, arrow[0]).astype(BF16).reshape(lat_count, 2, share // 2, share)
    panel = jnp.swapaxes(panel, 1, 2).reshape(lat_count, share // 2, 2 * share)
    panel_rows = lax.all_to_all(panel, "lat", 0, 0)
    everyone = range(depth_count)
    first = pack(ring_gather(pair, everyone, False))
    blocks = ring_gather(first, everyone, True)
    order = jnp.stack(order)
    step, bias = step_terms(order, panel_rows, blocks)
    swap = [(d, d ^ 1) for d in range(depth_count)]
    got = lax.ppermute(step, "depth", swap)
    bias_got = lax.ppermute(bias, "depth", [(2 * k, 2 * k + 1) for k in range(chips)])
    product, step_odd, add_even = products(core, step, got, bias, bias_got)
    add_odd = jnp.where(low, jnp.zeros_like(bias), bias)
    lower = (chips * 6) // 16
    tops = [chips - 1, lower - 1]
    sizes = [chips - lower, lower]
    start = (row == col) & ((chip == tops[0]) | (chip == tops[1])) & low
    v_in = jnp.where(start, 1.0, 0.0).astype(BF16)
    v_even = mm(v_in, product) + add_even
    for hop in range(1, max(sizes)):
        pairs = []
        for block_top, size, cores in zip(tops, sizes, ((1,), (0, 1))):
            if hop < size:
                source = block_top - hop + 1
                pairs += [(2 * source + k, 2 * source - 2 + k) for k in cores]
        v_in = v_in + lax.ppermute(v_even.astype(BF16), "depth", pairs)
        v_even = mm(v_in, product) + add_even
    edge = v_even.astype(BF16)
    v_odd = mm(v_in, step_odd) + add_odd
    other = lax.ppermute(
        jnp.where(low, v_odd.astype(BF16), edge), "depth", swap[: 2 * lower]
    )
    map_rows = jnp.where(low, edge, other)
    depths = range(2 * lower)
    ring = jnp.concatenate(ring_gather(map_rows, depths, False))
    near, far = lower - 1, lower // 2 - 1
    entry = joined(sent_down(edge, [(lower, near)]), sent_down(edge, [(lower, far)]), ring)
    relayed = sent_down(entry, [(near, near - 1), (far, far - 1)])
    last = [(source, source - 2) for source, low_end in ((near, far), (far, -1)) if source - 2 > low_end]
    last = sent_down(entry, last)
    maps = place(order, ring_gather(ring, depths, True))
    below = chip < lower
    flags = jnp.stack([low, below]).astype(jnp.int32)
    entry = settled(flags, entry, relayed, last, edge)
    across = lax.ppermute(entry, "depth", [(2 * k + 1, 2 * k) for k in range(chips)])
    return closed(flags, maps, entry, across, other, v_odd)[None]


def solution(mesh):
    placed = (
        P("depth", "lat", None),
        P("depth", None, "lat"),
        P("depth", None, "lat"),
        P(),
        P("depth"),
    )
    return jax.shard_map(
        body, mesh=mesh, in_specs=placed, out_specs=P("depth", "lat", None), check_vma=False
    )
```

```python
import jax
import jax.numpy as jnp
from jax import lax
from jax.experimental import pallas as pl
from jax.experimental.pallas import tpu as pltpu
from jax.sharding import PartitionSpec as P

HALF = 512
BOTH = ("depth", "lat")
F32 = jnp.float32
BF16 = jnp.bfloat16
SIDE = 4
VMEM = pl.BlockSpec(memory_space=pltpu.VMEM)
SMEM = pl.BlockSpec(memory_space=pltpu.SMEM)
MIB = 1024 * 1024
PARAMS = pltpu.CompilerParams(vmem_limit_bytes=16 * MIB)
SMALL = pltpu.CompilerParams(vmem_limit_bytes=4 * MIB)


def mm(a, b):
    return jnp.dot(a, b, preferred_element_type=F32)


def around(base):
    return [(base + shift) % SIDE for shift in (0, -1, 1, 2)]


def ring_moves(depths, flipped, shift):
    pairs = []
    for d in depths:
        by_x = (d % 2 == 0) != flipped
        for y in range(SIDE):
            for x in range(SIDE):
                ty, tx = (y, (x + shift) % SIDE) if by_x else ((y + shift) % SIDE, x)
                pairs.append(((d * SIDE + y) * SIDE + x, (d * SIDE + ty) * SIDE + tx))
    return pairs


def ring_gather(value, depths, flipped):
    return [value] + [
        lax.ppermute(value, BOTH, ring_moves(depths, flipped, shift))
        for shift in (1, -1, 2)
    ]


def sent_down(value, chip_pairs):
    return lax.ppermute(value, "depth", [(2 * a + 1, 2 * b + 1) for a, b in chip_pairs])


def place_kernel(order, a, b, c, d, out):
    count = out.shape[0] // 16
    for g, block in enumerate((a, b, c, d)):
        for f in range(4):
            start = pl.multiple_of(order[4 * g + f] * count, count)
            out[pl.ds(start, count), :] = block[f * count : (f + 1) * count, :]


def place(order, blocks):
    rows, width = blocks[0].shape
    return pl.pallas_call(
        place_kernel,
        out_shape=jax.ShapeDtypeStruct((4 * rows, width), blocks[0].dtype),
        in_specs=[SMEM] + [VMEM] * 4,
        out_specs=VMEM,
        compiler_params=PARAMS,
    )(order, *blocks)


def pack_kernel(a, b, c, d, out):
    count = a.shape[1]
    wide = out.shape[1]
    for f, block in enumerate((a, b, c, d)):
        out[0, f * count : (f + 1) * count, :] = block[0]
    for m in range(a.shape[2] // wide):
        cut = slice(m * wide, (m + 1) * wide)
        turned = jnp.concatenate([block[1, :, cut] for block in (a, b, c, d)])
        out[1, :, cut] = turned.T


def pack(blocks):
    two, count, width = blocks[0].shape
    return pl.pallas_call(
        pack_kernel,
        out_shape=jax.ShapeDtypeStruct((two, 4 * count, width), BF16),
        in_specs=[VMEM] * 4,
        out_specs=VMEM,
        compiler_params=PARAMS,
    )(*blocks)


def half_product(first, second, cut):
    left = jnp.concatenate([first[1, :, cut], second[1, :, cut]], axis=1)
    return mm(left, jnp.concatenate([first[0], second[0]]))


def part_kernel(a, d, out, token):
    token[...] = jnp.zeros_like(token)
    wide = a.shape[1]
    for m in range(out.shape[0] // wide):
        cut = slice(m * wide, (m + 1) * wide)
        out[cut, :] = half_product(a, d, cut).astype(BF16)


def step_kernel(part, b, c, step, token):
    token[...] = jnp.zeros_like(token)
    wide = b.shape[1]
    for m in range(step.shape[0] // wide):
        cut = slice(m * wide, (m + 1) * wide)
        step[cut, :] = (-(part[cut, :].astype(F32) + half_product(b, c, cut))).astype(BF16)


def bias_kernel(panel, a, b, c, d, bias):
    wide = a.shape[1]
    total = mm(panel[:, :wide], a[0])
    for f, right in ((1, b), (2, c), (3, d)):
        total = total + mm(panel[:, f * wide : (f + 1) * wide], right[0])
    bias[...] = -total


def cut_kernel(order, panel, ready, out):
    share = panel.shape[2] // 2
    for i in range(0, panel.shape[0], 2):
        two = [panel[order[i]].astype(F32), panel[order[i + 1]].astype(F32)]
        upper = jnp.concatenate([part[:, :share] for part in two], axis=1)
        under = jnp.concatenate([part[:, share:] for part in two], axis=1)
        both = jnp.concatenate([upper, under]).astype(BF16)
        out[:, i * share : (i + 2) * share] = both


def step_terms(order, panel, blocks):
    a, b, c, d = blocks
    two, wide, width = a.shape
    whole = jax.ShapeDtypeStruct((width, width), BF16)
    token = jax.ShapeDtypeStruct((8, 128), F32)
    part, unused = pl.pallas_call(
        part_kernel,
        out_shape=[whole, token],
        in_specs=[VMEM] * 2,
        out_specs=[VMEM, VMEM],
        compiler_params=PARAMS,
    )(a, d)
    step, ready = pl.pallas_call(
        step_kernel,
        out_shape=[whole, token],
        in_specs=[VMEM] * 3,
        out_specs=[VMEM, VMEM],
        compiler_params=PARAMS,
    )(part, b, c)
    rows = 2 * panel.shape[1]
    panel = pl.pallas_call(
        cut_kernel,
        out_shape=jax.ShapeDtypeStruct((rows, width), BF16),
        in_specs=[SMEM, VMEM, VMEM],
        out_specs=VMEM,
        compiler_params=SMALL,
    )(order, panel, ready)
    flat = pl.BlockSpec((rows, width), lambda i: (0, 0))
    bias = pl.pallas_call(
        bias_kernel,
        out_shape=jax.ShapeDtypeStruct((rows, width), F32),
        in_specs=[flat] + [pl.BlockSpec((1, wide, width), lambda i: (0, 0, 0))] * 4,
        out_specs=flat,
        grid=(1,),
        compiler_params=PARAMS,
        cost_estimate=pl.CostEstimate(flops=40 * width**3, bytes_accessed=6 * width**2, transcendentals=0),
    )(panel, a, b, c, d)
    return step, bias


def product_kernel(core, own, got, bias, bias_got, product, odd, add_even, turn):
    turn[...] = jnp.zeros_like(turn)
    cut = 256
    width = own.shape[0]

    def fill(first, second):
        for m in range(width // cut):
            rows = slice(m * cut, (m + 1) * cut)
            product[rows, :] = mm(first[rows, :], second[...]).astype(BF16)
        odd[...] = first[...]

    @pl.when(core[0] == 0)
    def _():
        fill(got, own)
        add_even[...] = jnp.zeros_like(add_even)

    @pl.when(core[0] != 0)
    def _():
        fill(own, got)
        add_even[...] = mm(bias[...].astype(BF16), got[...]) + bias_got[...]


def products(core, own, got, bias, bias_got):
    width = own.shape[0]
    return pl.pallas_call(
        product_kernel,
        out_shape=[
            jax.ShapeDtypeStruct(own.shape, BF16),
            jax.ShapeDtypeStruct(own.shape, BF16),
            jax.ShapeDtypeStruct(bias.shape, F32),
            jax.ShapeDtypeStruct((8, 128), F32),
        ],
        in_specs=[SMEM] + [VMEM] * 4,
        out_specs=[VMEM] * 4,
        compiler_params=PARAMS,
        cost_estimate=pl.CostEstimate(flops=2 * width**3, bytes_accessed=6 * width**2, transcendentals=0),
    )(core.reshape(1), own, got, bias, bias_got)


def hold_kernel(value, ready, out):
    out[...] = value[...]


def held(value, ready):
    return pl.pallas_call(
        hold_kernel,
        out_shape=jax.ShapeDtypeStruct(value.shape, value.dtype),
        in_specs=[VMEM, VMEM],
        out_specs=VMEM,
        compiler_params=SMALL,
    )(value, ready)


def join_kernel(a, b, ready, out):
    out[...] = a[...] + b[...]


def joined(a, b, ready):
    return pl.pallas_call(
        join_kernel,
        out_shape=jax.ShapeDtypeStruct(a.shape, a.dtype),
        in_specs=[VMEM, VMEM, VMEM],
        out_specs=VMEM,
        compiler_params=SMALL,
        cost_estimate=pl.CostEstimate(flops=4 * 10**10, bytes_accessed=0, transcendentals=0),
    )(a, b, ready)


def settle_kernel(flags, entry, relayed, last, edge, out):
    @pl.when(flags[1] != 0)
    def _():
        out[...] = entry[...] + relayed[...] + last[...]

    @pl.when(flags[1] == 0)
    def _():
        out[...] = edge[...]


def settled(flags, entry, relayed, last, edge):
    return pl.pallas_call(
        settle_kernel,
        out_shape=jax.ShapeDtypeStruct(entry.shape, entry.dtype),
        in_specs=[SMEM] + [VMEM] * 4,
        out_specs=VMEM,
        compiler_params=SMALL,
    )(flags, entry, relayed, last, edge)


def close_kernel(flags, maps, entry, across, other, v_odd, out):
    low, below = flags[0] != 0, flags[1] != 0

    @pl.when(low & below)
    def _():
        out[...] = mm(across[...], maps[...]) + other[...].astype(F32)

    @pl.when(low & jnp.logical_not(below))
    def _():
        out[...] = across[...].astype(F32)

    @pl.when(jnp.logical_not(low) & below)
    def _():
        out[...] = mm(entry[...], maps[...]) + v_odd[...]

    @pl.when(jnp.logical_not(low) & jnp.logical_not(below))
    def _():
        out[...] = v_odd[...]


def closed(flags, maps, entry, across, other, v_odd):
    return pl.pallas_call(
        close_kernel,
        out_shape=jax.ShapeDtypeStruct(entry.shape, F32),
        in_specs=[SMEM] + [VMEM] * 5,
        out_specs=VMEM,
        compiler_params=PARAMS,
    )(flags, maps, entry, across, other, v_odd)


def body(inv_diag, couple, arrow, corner, band_offset):
    depth_count = lax.axis_size("depth")
    lat_count = lax.axis_size("lat")
    depth = lax.axis_index("depth")
    lat = lax.axis_index("lat")
    core = depth % 2
    chip = depth // 2
    chips = depth_count // 2
    low = core == 0
    y, x = lat // SIDE, lat % SIDE
    order = [
        jnp.where(low, SIDE * b + a, SIDE * a + b)
        for b in around(jnp.where(low, y, x))
        for a in around(jnp.where(low, x, y))
    ]
    g_rows = inv_diag[0]
    share, width = g_rows.shape
    cells = couple[0].T
    row = lax.broadcasted_iota(jnp.int32, cells.shape, 0) + lat * share
    col = lax.broadcasted_iota(jnp.int32, cells.shape, 1)
    keep = jnp.abs(row - col - band_offset[0]) <= HALF
    pair = jnp.stack([g_rows, jnp.where(keep, cells, jnp.zeros_like(cells))])
    panel = mm(corner, arrow[0]).astype(BF16).reshape(lat_count, 2, share // 2, share)
    panel = jnp.swapaxes(panel, 1, 2).reshape(lat_count, share // 2, 2 * share)
    panel_rows = lax.all_to_all(panel, "lat", 0, 0)
    everyone = range(depth_count)
    first = pack(ring_gather(pair, everyone, False))
    blocks = ring_gather(first, everyone, True)
    order = jnp.stack(order)
    step, bias = step_terms(order, panel_rows, blocks)
    swap = [(d, d ^ 1) for d in range(depth_count)]
    got = lax.ppermute(step, "depth", swap)
    bias_got = lax.ppermute(bias, "depth", [(2 * k, 2 * k + 1) for k in range(chips)])
    product, step_odd, add_even, turn = products(core, step, got, bias, bias_got)
    add_odd = jnp.where(low, jnp.zeros_like(bias), bias)
    lower = (chips * 6) // 16
    tops = [chips - 1, lower - 1]
    sizes = [chips - lower, lower]
    start = (row == col) & ((chip == tops[0]) | (chip == tops[1])) & low
    v_in = jnp.where(start, 1.0, 0.0).astype(BF16)
    turn = lax.ppermute(turn, "depth", [(2 * k, 2 * k + 1) for k in range(lower)])
    v_in = held(v_in, turn)
    v_even = mm(v_in, product) + add_even
    for hop in range(1, max(sizes)):
        pairs = []
        for block_top, size, cores in zip(tops, sizes, ((1,), (0, 1))):
            if hop < size:
                source = block_top - hop + 1
                pairs += [(2 * source + k, 2 * source - 2 + k) for k in cores]
        v_in = v_in + lax.ppermute(v_even.astype(BF16), "depth", pairs)
        v_even = mm(v_in, product) + add_even
    edge = v_even.astype(BF16)
    v_odd = mm(v_in, step_odd) + add_odd
    other = lax.ppermute(
        jnp.where(low, v_odd.astype(BF16), edge), "depth", swap[: 2 * lower]
    )
    map_rows = jnp.where(low, edge, other)
    depths = range(2 * lower)
    ring = jnp.concatenate(ring_gather(map_rows, depths, False))
    near, far = lower - 1, lower // 2 - 1
    entry = joined(sent_down(edge, [(lower, near)]), sent_down(edge, [(lower, far)]), ring)
    relayed = sent_down(entry, [(near, near - 1), (far, far - 1)])
    last = [(source, source - 2) for source, low_end in ((near, far), (far, -1)) if source - 2 > low_end]
    last = sent_down(entry, last)
    maps = place(order, ring_gather(ring, depths, True))
    below = chip < lower
    flags = jnp.stack([low, below]).astype(jnp.int32)
    entry = settled(flags, entry, relayed, last, edge)
    across = lax.ppermute(entry, "depth", [(2 * k + 1, 2 * k) for k in range(chips)])
    return closed(flags, maps, entry, across, other, v_odd)[None]


def solution(mesh):
    placed = (
        P("depth", "lat", None),
        P("depth", None, "lat"),
        P("depth", None, "lat"),
        P(),
        P("depth"),
    )
    return jax.shard_map(
        body, mesh=mesh, in_specs=placed, out_specs=P("depth", "lat", None), check_vma=False
    )
```

```python
import jax
import jax.numpy as jnp
from jax import lax
from jax.experimental import pallas as pl
from jax.experimental.pallas import tpu as pltpu
from jax.sharding import PartitionSpec as P

HALF = 512
BOTH = ("depth", "lat")
F32 = jnp.float32
BF16 = jnp.bfloat16
SIDE = 4
VMEM = pl.BlockSpec(memory_space=pltpu.VMEM)
SMEM = pl.BlockSpec(memory_space=pltpu.SMEM)
MIB = 1024 * 1024
PARAMS = pltpu.CompilerParams(vmem_limit_bytes=16 * MIB)
SMALL = pltpu.CompilerParams(vmem_limit_bytes=4 * MIB)


def mm(a, b):
    return jnp.dot(a, b, preferred_element_type=F32)


def around(base):
    return [(base + shift) % SIDE for shift in (0, -1, 1, 2)]


def ring_moves(depths, flipped, shift):
    pairs = []
    for d in depths:
        by_x = (d % 2 == 0) != flipped
        for y in range(SIDE):
            for x in range(SIDE):
                ty, tx = (y, (x + shift) % SIDE) if by_x else ((y + shift) % SIDE, x)
                pairs.append(((d * SIDE + y) * SIDE + x, (d * SIDE + ty) * SIDE + tx))
    return pairs


def ring_gather(value, depths, flipped):
    return [value] + [
        lax.ppermute(value, BOTH, ring_moves(depths, flipped, shift))
        for shift in (1, -1, 2)
    ]


def sent_down(value, chip_pairs):
    return lax.ppermute(value, "depth", [(2 * a + 1, 2 * b + 1) for a, b in chip_pairs])


def pack_kernel(a, b, c, d, out):
    count = a.shape[1]
    wide = out.shape[1]
    for f, block in enumerate((a, b, c, d)):
        out[0, f * count : (f + 1) * count, :] = block[0]
    for m in range(a.shape[2] // wide):
        cut = slice(m * wide, (m + 1) * wide)
        turned = jnp.concatenate([block[1, :, cut] for block in (a, b, c, d)])
        out[1, :, cut] = turned.T


def pack(blocks):
    two, count, width = blocks[0].shape
    return pl.pallas_call(
        pack_kernel,
        out_shape=jax.ShapeDtypeStruct((two, 4 * count, width), BF16),
        in_specs=[VMEM] * 4,
        out_specs=VMEM,
        compiler_params=PARAMS,
    )(*blocks)


def half_product(first, second, cut):
    left = jnp.concatenate([first[1, :, cut], second[1, :, cut]], axis=1)
    return mm(left, jnp.concatenate([first[0], second[0]]))


def part_kernel(a, d, out, token):
    token[...] = jnp.zeros_like(token)
    wide = a.shape[1]
    for m in range(out.shape[0] // wide):
        cut = slice(m * wide, (m + 1) * wide)
        out[cut, :] = half_product(a, d, cut).astype(BF16)


def step_kernel(part, b_left, b_right, c_left, c_right, step, token):
    token[...] = jnp.zeros_like(token)
    left = jnp.concatenate([b_left[0], c_left[0]], axis=1)
    right = jnp.concatenate([b_right[0], c_right[0]])
    step[...] = (-(part[...].astype(F32) + mm(left, right))).astype(BF16)


def bias_kernel(panel, a, b, c, d, bias):
    wide = a.shape[1]
    total = mm(panel[:, :wide], a[0])
    for f, right in ((1, b), (2, c), (3, d)):
        total = total + mm(panel[:, f * wide : (f + 1) * wide], right[0])
    bias[...] = -total


def cut_kernel(order, panel, ready, out):
    share = panel.shape[2] // 2
    for i in range(0, panel.shape[0], 2):
        two = [panel[order[i]].astype(F32), panel[order[i + 1]].astype(F32)]
        upper = jnp.concatenate([part[:, :share] for part in two], axis=1)
        under = jnp.concatenate([part[:, share:] for part in two], axis=1)
        both = jnp.concatenate([upper, under]).astype(BF16)
        out[:, i * share : (i + 2) * share] = both


def step_terms(order, panel, blocks):
    a, b, c, d = blocks
    two, wide, width = a.shape
    whole = jax.ShapeDtypeStruct((width, width), BF16)
    token = jax.ShapeDtypeStruct((8, 128), F32)
    part, unused = pl.pallas_call(
        part_kernel,
        out_shape=[whole, token],
        in_specs=[VMEM] * 2,
        out_specs=[VMEM, VMEM],
        compiler_params=PARAMS,
    )(a, d)
    rows_of = pl.BlockSpec((wide, width), lambda m: (m, 0))
    left = pl.BlockSpec((1, wide, wide), lambda m: (1, 0, m))
    right = pl.BlockSpec((1, wide, width), lambda m: (0, 0, 0))
    step, ready = pl.pallas_call(
        step_kernel,
        out_shape=[whole, token],
        grid=(width // wide,),
        in_specs=[rows_of, left, right, left, right],
        out_specs=[rows_of, pl.BlockSpec((8, 128), lambda m: (0, 0))],
        compiler_params=PARAMS,
    )(part, b, b, c, c)
    rows = 2 * panel.shape[1]
    panel = pl.pallas_call(
        cut_kernel,
        out_shape=jax.ShapeDtypeStruct((rows, width), BF16),
        in_specs=[SMEM, VMEM, VMEM],
        out_specs=VMEM,
        compiler_params=SMALL,
    )(order, panel, ready)
    flat = pl.BlockSpec((rows, width), lambda i: (0, 0))
    bias = pl.pallas_call(
        bias_kernel,
        out_shape=jax.ShapeDtypeStruct((rows, width), F32),
        in_specs=[flat] + [pl.BlockSpec((1, wide, width), lambda i: (0, 0, 0))] * 4,
        out_specs=flat,
        grid=(1,),
        compiler_params=PARAMS,
        cost_estimate=pl.CostEstimate(flops=40 * width**3, bytes_accessed=6 * width**2, transcendentals=0),
    )(panel, a, b, c, d)
    return step, bias


def product_kernel(core, own, got, bias, bias_got, product, odd, add_even):
    cut = 256
    width = own.shape[0]

    def fill(first, second):
        for m in range(width // cut):
            rows = slice(m * cut, (m + 1) * cut)
            product[rows, :] = mm(first[rows, :], second[...]).astype(BF16)
        odd[...] = first[...]

    @pl.when(core[0] == 0)
    def _():
        fill(got, own)
        add_even[...] = jnp.zeros_like(add_even)

    @pl.when(core[0] != 0)
    def _():
        fill(own, got)
        add_even[...] = mm(bias[...].astype(BF16), got[...]) + bias_got[...]


def products(core, own, got, bias, bias_got):
    width = own.shape[0]
    return pl.pallas_call(
        product_kernel,
        out_shape=[
            jax.ShapeDtypeStruct(own.shape, BF16),
            jax.ShapeDtypeStruct(own.shape, BF16),
            jax.ShapeDtypeStruct(bias.shape, F32),
        ],
        in_specs=[SMEM] + [VMEM] * 4,
        out_specs=[VMEM] * 3,
        compiler_params=PARAMS,
        cost_estimate=pl.CostEstimate(flops=2 * width**3, bytes_accessed=6 * width**2, transcendentals=0),
    )(core.reshape(1), own, got, bias, bias_got)


def join_kernel(a, b, ready, out):
    out[...] = a[...] + b[...]


def joined(a, b, ready):
    return pl.pallas_call(
        join_kernel,
        out_shape=jax.ShapeDtypeStruct(a.shape, a.dtype),
        in_specs=[VMEM, VMEM, VMEM],
        out_specs=VMEM,
        compiler_params=SMALL,
    )(a, b, ready)


def settle_kernel(flags, entry, relayed, last, edge, out):
    @pl.when(flags[1] != 0)
    def _():
        out[...] = entry[...] + relayed[...] + last[...]

    @pl.when(flags[1] == 0)
    def _():
        out[...] = edge[...]


def settled(flags, entry, relayed, last, edge):
    return pl.pallas_call(
        settle_kernel,
        out_shape=jax.ShapeDtypeStruct(entry.shape, entry.dtype),
        in_specs=[SMEM] + [VMEM] * 4,
        out_specs=VMEM,
        compiler_params=SMALL,
    )(flags, entry, relayed, last, edge)


def close_kernel(flags, order, a, b, c, d, entry, across, other, v_odd, out, maps, sems):
    low, below = flags[0] != 0, flags[1] != 0
    count = maps.shape[0] // 16

    @pl.when(below)
    def _():
        copies = []
        for g, block in enumerate((a, b, c, d)):
            for f in range(4):
                start = pl.multiple_of(order[4 * g + f] * count, count)
                copies.append(
                    pltpu.make_async_copy(
                        block.at[pl.ds(f * count, count), :],
                        maps.at[pl.ds(start, count), :],
                        sems.at[4 * g + f],
                    )
                )
        for copy in copies:
            copy.start()
        for copy in copies:
            copy.wait()

    @pl.when(low & below)
    def _():
        out[...] = mm(across[...], maps[...]) + other[...].astype(F32)

    @pl.when(low & jnp.logical_not(below))
    def _():
        out[...] = across[...].astype(F32)

    @pl.when(jnp.logical_not(low) & below)
    def _():
        out[...] = mm(entry[...], maps[...]) + v_odd[...]

    @pl.when(jnp.logical_not(low) & jnp.logical_not(below))
    def _():
        out[...] = v_odd[...]


def closed(flags, order, blocks, entry, across, other, v_odd):
    width = entry.shape[1]
    return pl.pallas_call(
        close_kernel,
        out_shape=jax.ShapeDtypeStruct(entry.shape, F32),
        in_specs=[SMEM, SMEM] + [pl.BlockSpec(memory_space=pl.ANY)] * 4 + [VMEM] * 4,
        out_specs=VMEM,
        scratch_shapes=[pltpu.VMEM((width, width), BF16), pltpu.SemaphoreType.DMA((16,))],
        compiler_params=PARAMS,
    )(flags, order, *blocks, entry, across, other, v_odd)


def body(inv_diag, couple, arrow, corner, band_offset):
    depth_count = lax.axis_size("depth")
    lat_count = lax.axis_size("lat")
    depth = lax.axis_index("depth")
    lat = lax.axis_index("lat")
    core = depth % 2
    chip = depth // 2
    chips = depth_count // 2
    low = core == 0
    y, x = lat // SIDE, lat % SIDE
    order = [
        jnp.where(low, SIDE * b + a, SIDE * a + b)
        for b in around(jnp.where(low, y, x))
        for a in around(jnp.where(low, x, y))
    ]
    g_rows = inv_diag[0]
    share, width = g_rows.shape
    cells = couple[0].T
    row = lax.broadcasted_iota(jnp.int32, cells.shape, 0) + lat * share
    col = lax.broadcasted_iota(jnp.int32, cells.shape, 1)
    keep = jnp.abs(row - col - band_offset[0]) <= HALF
    pair = jnp.stack([g_rows, jnp.where(keep, cells, jnp.zeros_like(cells))])
    panel = mm(corner, arrow[0]).astype(BF16).reshape(lat_count, 2, share // 2, share)
    panel = jnp.swapaxes(panel, 1, 2).reshape(lat_count, share // 2, 2 * share)
    panel_rows = lax.all_to_all(panel, "lat", 0, 0)
    everyone = range(depth_count)
    first = pack(ring_gather(pair, everyone, False))
    blocks = ring_gather(first, everyone, True)
    order = jnp.stack(order)
    step, bias = step_terms(order, panel_rows, blocks)
    swap = [(d, d ^ 1) for d in range(depth_count)]
    got = lax.ppermute(step, "depth", swap)
    bias_got = lax.ppermute(bias, "depth", [(2 * k, 2 * k + 1) for k in range(chips)])
    product, step_odd, add_even = products(core, step, got, bias, bias_got)
    add_odd = jnp.where(low, jnp.zeros_like(bias), bias)
    lower = (chips * 6) // 16
    tops = [chips - 1, lower - 1]
    sizes = [chips - lower, lower]
    start = (row == col) & ((chip == tops[0]) | (chip == tops[1])) & low
    v_in = jnp.where(start, 1.0, 0.0).astype(BF16)
    v_even = mm(v_in, product) + add_even
    for hop in range(1, max(sizes)):
        pairs = []
        for block_top, size, cores in zip(tops, sizes, ((1,), (0, 1))):
            if hop < size:
                source = block_top - hop + 1
                pairs += [(2 * source + k, 2 * source - 2 + k) for k in cores]
        v_in = v_in + lax.ppermute(v_even.astype(BF16), "depth", pairs)
        v_even = mm(v_in, product) + add_even
    edge = v_even.astype(BF16)
    v_odd = mm(v_in, step_odd) + add_odd
    other = lax.ppermute(
        jnp.where(low, v_odd.astype(BF16), edge), "depth", swap[: 2 * lower]
    )
    map_rows = jnp.where(low, edge, other)
    depths = range(2 * lower)
    ring = jnp.concatenate(ring_gather(map_rows, depths, False))
    near, far = lower - 1, lower // 2 - 1
    entry = joined(sent_down(edge, [(lower, near)]), sent_down(edge, [(lower, far)]), ring)
    relayed = sent_down(entry, [(near, near - 1), (far, far - 1)])
    last = [(source, source - 2) for source, low_end in ((near, far), (far, -1)) if source - 2 > low_end]
    last = sent_down(entry, last)
    blocks = ring_gather(ring, depths, True)
    below = chip < lower
    flags = jnp.stack([low, below]).astype(jnp.int32)
    entry = settled(flags, entry, relayed, last, edge)
    across = lax.ppermute(entry, "depth", [(2 * k + 1, 2 * k) for k in range(chips)])
    return closed(flags, order, blocks, entry, across, other, v_odd)[None]


def solution(mesh):
    placed = (
        P("depth", "lat", None),
        P("depth", None, "lat"),
        P("depth", None, "lat"),
        P(),
        P("depth"),
    )
    return jax.shard_map(
        body, mesh=mesh, in_specs=placed, out_specs=P("depth", "lat", None), check_vma=False
    )
```

```python
import jax
import jax.numpy as jnp
from jax import lax
from jax.experimental import pallas as pl
from jax.experimental.pallas import tpu as pltpu
from jax.sharding import PartitionSpec as P

HALF = 512
BOTH = ("depth", "lat")
F32 = jnp.float32
BF16 = jnp.bfloat16
SIDE = 4
VMEM = pl.BlockSpec(memory_space=pltpu.VMEM)
SMEM = pl.BlockSpec(memory_space=pltpu.SMEM)
MIB = 1024 * 1024


def room(mib):
    return pltpu.CompilerParams(vmem_limit_bytes=mib * MIB)


SMALL = pltpu.CompilerParams(vmem_limit_bytes=2 * MIB)


def mm(a, b):
    return jnp.dot(a, b, preferred_element_type=F32)


def around(base):
    return [(base + shift) % SIDE for shift in (0, -1, 1, 2)]


def ring_moves(depths, flipped, shift):
    pairs = []
    for d in depths:
        by_x = (d % 2 == 0) != flipped
        for y in range(SIDE):
            for x in range(SIDE):
                ty, tx = (y, (x + shift) % SIDE) if by_x else ((y + shift) % SIDE, x)
                pairs.append(((d * SIDE + y) * SIDE + x, (d * SIDE + ty) * SIDE + tx))
    return pairs


def ring_gather(value, depths, flipped):
    from_right, from_left, across = [
        lax.ppermute(value, BOTH, ring_moves(depths, flipped, shift))
        for shift in (-1, 1, 2)
    ]
    return [value, from_left, from_right, across]


def sent_down(value, chip_pairs):
    return lax.ppermute(value, "depth", [(2 * a + 1, 2 * b + 1) for a, b in chip_pairs])


def place_kernel(order, a, b, c, d, out):
    count = out.shape[0] // 16
    for g, block in enumerate((a, b, c, d)):
        for f in range(4):
            start = pl.multiple_of(order[4 * g + f] * count, count)
            out[pl.ds(start, count), :] = block[f * count : (f + 1) * count, :]


def place(order, blocks):
    rows, width = blocks[0].shape
    return pl.pallas_call(
        place_kernel,
        out_shape=jax.ShapeDtypeStruct((4 * rows, width), blocks[0].dtype),
        in_specs=[SMEM] + [VMEM] * 4,
        out_specs=VMEM,
        compiler_params=room(6),
    )(order, *blocks)


def pack_kernel(a, b, c, d, out):
    count = a.shape[1]
    wide = out.shape[1]
    for f, block in enumerate((a, b, c, d)):
        out[0, f * count : (f + 1) * count, :] = block[0]
    for m in range(a.shape[2] // wide):
        cut = slice(m * wide, (m + 1) * wide)
        turned = jnp.concatenate([block[1, :, cut] for block in (a, b, c, d)])
        out[1, :, cut] = turned.T


def pack(blocks):
    two, count, width = blocks[0].shape
    return pl.pallas_call(
        pack_kernel,
        out_shape=jax.ShapeDtypeStruct((two, 4 * count, width), BF16),
        in_specs=[VMEM] * 4,
        out_specs=VMEM,
        compiler_params=room(6),
    )(*blocks)


def half_product(first, second, cut):
    left = jnp.concatenate([first[1, :, cut], second[1, :, cut]], axis=1)
    return mm(left, jnp.concatenate([first[0], second[0]]))


def part_kernel(a, d, out, token):
    token[...] = jnp.zeros_like(token)
    wide = a.shape[1]
    for m in range(out.shape[0] // wide):
        cut = slice(m * wide, (m + 1) * wide)
        out[cut, :] = half_product(a, d, cut).astype(BF16)


def step_kernel(part, b, c, step, token):
    token[...] = jnp.zeros_like(token)
    wide = b.shape[1]
    for m in range(step.shape[0] // wide):
        cut = slice(m * wide, (m + 1) * wide)
        step[cut, :] = (-(part[cut, :].astype(F32) + half_product(b, c, cut))).astype(BF16)


def bias_kernel(panel, a, b, c, d, bias):
    wide = a.shape[1]
    total = mm(panel[:, :wide], a[0])
    for f, right in ((1, b), (2, c), (3, d)):
        total = total + mm(panel[:, f * wide : (f + 1) * wide], right[0])
    bias[...] = -total


def cut_kernel(order, panel, ready, out):
    share = panel.shape[2] // 2
    for i in range(0, panel.shape[0], 2):
        two = [panel[order[i]].astype(F32), panel[order[i + 1]].astype(F32)]
        upper = jnp.concatenate([part[:, :share] for part in two], axis=1)
        under = jnp.concatenate([part[:, share:] for part in two], axis=1)
        both = jnp.concatenate([upper, under]).astype(BF16)
        out[:, i * share : (i + 2) * share] = both


def step_terms(order, panel, blocks):
    a, b, c, d = blocks
    two, wide, width = a.shape
    whole = jax.ShapeDtypeStruct((width, width), BF16)
    token = jax.ShapeDtypeStruct((8, 128), F32)
    part, unused = pl.pallas_call(
        part_kernel,
        out_shape=[whole, token],
        in_specs=[VMEM] * 2,
        out_specs=[VMEM, VMEM],
        compiler_params=room(10),
    )(a, d)
    step, ready = pl.pallas_call(
        step_kernel,
        out_shape=[whole, token],
        in_specs=[VMEM] * 3,
        out_specs=[VMEM, VMEM],
        compiler_params=room(12),
    )(part, c, b)
    rows = 2 * panel.shape[1]
    panel = pl.pallas_call(
        cut_kernel,
        out_shape=jax.ShapeDtypeStruct((rows, width), BF16),
        in_specs=[SMEM, VMEM, VMEM],
        out_specs=VMEM,
        compiler_params=SMALL,
    )(order, panel, ready)
    flat = pl.BlockSpec((rows, width), lambda i: (0, 0))
    bias = pl.pallas_call(
        bias_kernel,
        out_shape=jax.ShapeDtypeStruct((rows, width), F32),
        in_specs=[flat] + [pl.BlockSpec((1, wide, width), lambda i: (0, 0, 0))] * 4,
        out_specs=flat,
        grid=(1,),
        compiler_params=room(8),
        cost_estimate=pl.CostEstimate(flops=40 * width**3, bytes_accessed=6 * width**2, transcendentals=0),
    )(panel, a, b, c, d)
    return step, bias


def product_kernel(core, own, got, bias, bias_got, product, odd, add_even, turn):
    turn[...] = jnp.zeros_like(turn)
    cut = 256
    width = own.shape[0]

    def fill(first, second):
        for m in range(width // cut):
            rows = slice(m * cut, (m + 1) * cut)
            product[rows, :] = mm(first[rows, :], second[...]).astype(BF16)
        odd[...] = first[...]

    @pl.when(core[0] == 0)
    def _():
        fill(got, own)
        add_even[...] = jnp.zeros_like(add_even)

    @pl.when(core[0] != 0)
    def _():
        fill(own, got)
        add_even[...] = mm(bias[...].astype(BF16), got[...]) + bias_got[...]


def products(core, own, got, bias, bias_got):
    width = own.shape[0]
    return pl.pallas_call(
        product_kernel,
        out_shape=[
            jax.ShapeDtypeStruct(own.shape, BF16),
            jax.ShapeDtypeStruct(own.shape, BF16),
            jax.ShapeDtypeStruct(bias.shape, F32),
            jax.ShapeDtypeStruct((8, 128), F32),
        ],
        in_specs=[SMEM] + [VMEM] * 4,
        out_specs=[VMEM] * 4,
        compiler_params=room(14),
        cost_estimate=pl.CostEstimate(flops=2 * width**3, bytes_accessed=6 * width**2, transcendentals=0),
    )(core.reshape(1), own, got, bias, bias_got)


def hold_kernel(value, ready, out):
    out[...] = value[...]


def held(value, ready):
    return pl.pallas_call(
        hold_kernel,
        out_shape=jax.ShapeDtypeStruct(value.shape, value.dtype),
        in_specs=[VMEM, VMEM],
        out_specs=VMEM,
        compiler_params=SMALL,
    )(value, ready)


def join_kernel(a, b, ready, out):
    out[...] = a[...] + b[...]


def joined(a, b, ready):
    return pl.pallas_call(
        join_kernel,
        out_shape=jax.ShapeDtypeStruct(a.shape, a.dtype),
        in_specs=[VMEM, VMEM, VMEM],
        out_specs=VMEM,
        compiler_params=SMALL,
        cost_estimate=pl.CostEstimate(flops=4 * 10**10, bytes_accessed=0, transcendentals=0),
    )(a, b, ready)


def settle_kernel(flags, entry, relayed, last, edge, out):
    @pl.when(flags[1] != 0)
    def _():
        out[...] = entry[...] + relayed[...] + last[...]

    @pl.when(flags[1] == 0)
    def _():
        out[...] = edge[...]


def settled(flags, entry, relayed, last, edge):
    return pl.pallas_call(
        settle_kernel,
        out_shape=jax.ShapeDtypeStruct(entry.shape, entry.dtype),
        in_specs=[SMEM] + [VMEM] * 4,
        out_specs=VMEM,
        compiler_params=SMALL,
    )(flags, entry, relayed, last, edge)


def close_kernel(flags, maps, entry, across, other, v_odd, out):
    low, below = flags[0] != 0, flags[1] != 0

    @pl.when(low & below)
    def _():
        out[...] = mm(across[...], maps[...]) + other[...].astype(F32)

    @pl.when(low & jnp.logical_not(below))
    def _():
        out[...] = across[...].astype(F32)

    @pl.when(jnp.logical_not(low) & below)
    def _():
        out[...] = mm(entry[...], maps[...]) + v_odd[...]

    @pl.when(jnp.logical_not(low) & jnp.logical_not(below))
    def _():
        out[...] = v_odd[...]


def closed(flags, maps, entry, across, other, v_odd):
    return pl.pallas_call(
        close_kernel,
        out_shape=jax.ShapeDtypeStruct(entry.shape, F32),
        in_specs=[SMEM] + [VMEM] * 5,
        out_specs=VMEM,
        compiler_params=room(5),
    )(flags, maps, entry, across, other, v_odd)


def body(inv_diag, couple, arrow, corner, band_offset):
    depth_count = lax.axis_size("depth")
    lat_count = lax.axis_size("lat")
    depth = lax.axis_index("depth")
    lat = lax.axis_index("lat")
    core = depth % 2
    chip = depth // 2
    chips = depth_count // 2
    low = core == 0
    y, x = lat // SIDE, lat % SIDE
    order = [
        jnp.where(low, SIDE * b + a, SIDE * a + b)
        for b in around(jnp.where(low, y, x))
        for a in around(jnp.where(low, x, y))
    ]
    g_rows = inv_diag[0]
    share, width = g_rows.shape
    cells = couple[0].T
    row = lax.broadcasted_iota(jnp.int32, cells.shape, 0) + lat * share
    col = lax.broadcasted_iota(jnp.int32, cells.shape, 1)
    keep = jnp.abs(row - col - band_offset[0]) <= HALF
    pair = jnp.stack([g_rows, jnp.where(keep, cells, jnp.zeros_like(cells))])
    panel = mm(corner, arrow[0]).astype(BF16).reshape(lat_count, 2, share // 2, share)
    panel = jnp.swapaxes(panel, 1, 2).reshape(lat_count, share // 2, 2 * share)
    panel_rows = lax.all_to_all(panel, "lat", 0, 0)
    everyone = range(depth_count)
    first = pack(ring_gather(pair, everyone, False))
    blocks = ring_gather(first, everyone, True)
    order = jnp.stack(order)
    step, bias = step_terms(order, panel_rows, blocks)
    swap = [(d, d ^ 1) for d in range(depth_count)]
    got = lax.ppermute(step, "depth", swap)
    bias_got = lax.ppermute(bias, "depth", [(2 * k, 2 * k + 1) for k in range(chips)])
    product, step_odd, add_even, turn = products(core, step, got, bias, bias_got)
    add_odd = jnp.where(low, jnp.zeros_like(bias), bias)
    lower = (chips * 6) // 16
    tops = [chips - 1, lower - 1]
    sizes = [chips - lower, lower]
    start = (row == col) & ((chip == tops[0]) | (chip == tops[1])) & low
    v_in = jnp.where(start, 1.0, 0.0).astype(BF16)
    v_in = held(v_in, sent_down(turn, [(k + 1, k) for k in range(lower)]))
    v_even = mm(v_in, product) + add_even
    for hop in range(1, max(sizes)):
        pairs = []
        for block_top, size, cores in zip(tops, sizes, ((1,), (0, 1))):
            if hop < size:
                source = block_top - hop + 1
                pairs += [(2 * source + k, 2 * source - 2 + k) for k in cores]
        v_in = v_in + lax.ppermute(v_even.astype(BF16), "depth", pairs)
        v_even = mm(v_in, product) + add_even
    edge = v_even.astype(BF16)
    v_odd = mm(v_in, step_odd) + add_odd
    other = lax.ppermute(
        jnp.where(low, v_odd.astype(BF16), edge), "depth", swap[: 2 * lower]
    )
    map_rows = jnp.where(low, edge, other)
    depths = range(2 * lower)
    ring = jnp.concatenate(ring_gather(map_rows, depths, False))
    near, far = lower - 1, lower // 2 - 1
    to_far = sent_down(edge, [(lower, far)])
    entry = joined(to_far, sent_down(edge, [(lower, near)]), ring)
    relayed = sent_down(entry, [(near, near - 1), (far, far - 1)])
    last = [(source, source - 2) for source, low_end in ((near, far), (far, -1)) if source - 2 > low_end]
    last = sent_down(entry, last)
    maps = place(order, ring_gather(ring, depths, True))
    below = chip < lower
    flags = jnp.stack([low, below]).astype(jnp.int32)
    entry = settled(flags, entry, relayed, last, edge)
    across = lax.ppermute(entry, "depth", [(2 * k + 1, 2 * k) for k in range(chips)])
    return closed(flags, maps, entry, across, other, v_odd)[None]


def solution(mesh):
    placed = (
        P("depth", "lat", None),
        P("depth", None, "lat"),
        P("depth", None, "lat"),
        P(),
        P("depth"),
    )
    return jax.shard_map(
        body, mesh=mesh, in_specs=placed, out_specs=P("depth", "lat", None), check_vma=False
    )
```

```python
import jax
import jax.numpy as jnp
from jax import lax
from jax.experimental import pallas as pl
from jax.experimental.pallas import tpu as pltpu
from jax.sharding import PartitionSpec as P

HALF = 512
BOTH = ("depth", "lat")
F32 = jnp.float32
BF16 = jnp.bfloat16
SIDE = 4
VMEM = pl.BlockSpec(memory_space=pltpu.VMEM)
SMEM = pl.BlockSpec(memory_space=pltpu.SMEM)
MIB = 1024 * 1024


def room(mib):
    return pltpu.CompilerParams(vmem_limit_bytes=mib * MIB)


SMALL = pltpu.CompilerParams(vmem_limit_bytes=2 * MIB)


def mm(a, b):
    return jnp.dot(a, b, preferred_element_type=F32)


def around(base):
    return [(base + shift) % SIDE for shift in (0, -1, 1, 2)]


def ring_moves(depths, flipped, shift):
    pairs = []
    for d in depths:
        by_x = (d % 2 == 0) != flipped
        for y in range(SIDE):
            for x in range(SIDE):
                ty, tx = (y, (x + shift) % SIDE) if by_x else ((y + shift) % SIDE, x)
                pairs.append(((d * SIDE + y) * SIDE + x, (d * SIDE + ty) * SIDE + tx))
    return pairs


def ring_gather(value, depths, flipped):
    from_right, from_left, across = [
        lax.ppermute(value, BOTH, ring_moves(depths, flipped, shift))
        for shift in (-1, 1, 2)
    ]
    return [value, from_left, from_right, across]


def sent_down(value, chip_pairs):
    return lax.ppermute(value, "depth", [(2 * a + 1, 2 * b + 1) for a, b in chip_pairs])


def place_kernel(order, a, b, c, d, out):
    count = out.shape[0] // 16
    for g, block in enumerate((a, b, c, d)):
        for f in range(4):
            start = pl.multiple_of(order[4 * g + f] * count, count)
            out[pl.ds(start, count), :] = block[f * count : (f + 1) * count, :]


def place(order, blocks):
    rows, width = blocks[0].shape
    return pl.pallas_call(
        place_kernel,
        out_shape=jax.ShapeDtypeStruct((4 * rows, width), blocks[0].dtype),
        in_specs=[SMEM] + [VMEM] * 4,
        out_specs=VMEM,
        compiler_params=room(6),
    )(order, *blocks)


def pack_kernel(a, d, c, b, out):
    count = a.shape[1]
    wide = out.shape[1]
    for f, block in enumerate((a, b, c, d)):
        out[0, f * count : (f + 1) * count, :] = block[0]
    for m in range(a.shape[2] // wide):
        cut = slice(m * wide, (m + 1) * wide)
        turned = jnp.concatenate([block[1, :, cut] for block in (a, b, c, d)])
        out[1, :, cut] = turned.T


def pack(blocks):
    two, count, width = blocks[0].shape
    return pl.pallas_call(
        pack_kernel,
        out_shape=jax.ShapeDtypeStruct((two, 4 * count, width), BF16),
        in_specs=[VMEM] * 4,
        out_specs=VMEM,
        compiler_params=room(6),
    )(blocks[0], *blocks[:0:-1])


def half_product(first, second, cut):
    left = jnp.concatenate([first[1, :, cut], second[1, :, cut]], axis=1)
    return mm(left, jnp.concatenate([first[0], second[0]]))


def part_kernel(a, d, out, token):
    token[...] = jnp.zeros_like(token)
    wide = a.shape[1]
    for m in range(out.shape[0] // wide):
        cut = slice(m * wide, (m + 1) * wide)
        out[cut, :] = half_product(a, d, cut).astype(BF16)


def step_kernel(part, b, c, step, token):
    token[...] = jnp.zeros_like(token)
    wide = b.shape[1]
    for m in range(step.shape[0] // wide):
        cut = slice(m * wide, (m + 1) * wide)
        step[cut, :] = (-(part[cut, :].astype(F32) + half_product(b, c, cut))).astype(BF16)


def bias_kernel(panel, a, b, c, d, bias):
    wide = a.shape[1]
    total = mm(panel[:, :wide], a[0])
    for f, right in ((1, b), (2, c), (3, d)):
        total = total + mm(panel[:, f * wide : (f + 1) * wide], right[0])
    bias[...] = -total


def cut_kernel(order, panel, ready, out):
    share = panel.shape[2] // 2
    for i in range(0, panel.shape[0], 2):
        two = [panel[order[i]].astype(F32), panel[order[i + 1]].astype(F32)]
        upper = jnp.concatenate([part[:, :share] for part in two], axis=1)
        under = jnp.concatenate([part[:, share:] for part in two], axis=1)
        both = jnp.concatenate([upper, under]).astype(BF16)
        out[:, i * share : (i + 2) * share] = both


def step_terms(order, panel, blocks):
    a, b, c, d = blocks
    two, wide, width = a.shape
    whole = jax.ShapeDtypeStruct((width, width), BF16)
    token = jax.ShapeDtypeStruct((8, 128), F32)
    part, unused = pl.pallas_call(
        part_kernel,
        out_shape=[whole, token],
        in_specs=[VMEM] * 2,
        out_specs=[VMEM, VMEM],
        compiler_params=room(10),
    )(a, d)
    step, ready = pl.pallas_call(
        step_kernel,
        out_shape=[whole, token],
        in_specs=[VMEM] * 3,
        out_specs=[VMEM, VMEM],
        compiler_params=room(12),
    )(part, c, b)
    rows = 2 * panel.shape[1]
    panel = pl.pallas_call(
        cut_kernel,
        out_shape=jax.ShapeDtypeStruct((rows, width), BF16),
        in_specs=[SMEM, VMEM, VMEM],
        out_specs=VMEM,
        compiler_params=SMALL,
    )(order, panel, ready)
    flat = pl.BlockSpec((rows, width), lambda i: (0, 0))
    bias = pl.pallas_call(
        bias_kernel,
        out_shape=jax.ShapeDtypeStruct((rows, width), F32),
        in_specs=[flat] + [pl.BlockSpec((1, wide, width), lambda i: (0, 0, 0))] * 4,
        out_specs=flat,
        grid=(1,),
        compiler_params=room(8),
        cost_estimate=pl.CostEstimate(flops=40 * width**3, bytes_accessed=6 * width**2, transcendentals=0),
    )(panel, a, b, c, d)
    return step, bias


def product_kernel(core, own, got, bias, bias_got, product, odd, add_even, turn):
    turn[...] = jnp.zeros_like(turn)
    cut = 256
    width = own.shape[0]

    def fill(first, second):
        for m in range(width // cut):
            rows = slice(m * cut, (m + 1) * cut)
            product[rows, :] = mm(first[rows, :], second[...]).astype(BF16)
        odd[...] = first[...]

    @pl.when(core[0] == 0)
    def _():
        fill(got, own)
        add_even[...] = jnp.zeros_like(add_even)

    @pl.when(core[0] != 0)
    def _():
        fill(own, got)
        add_even[...] = mm(bias[...].astype(BF16), got[...]) + bias_got[...]


def products(core, own, got, bias, bias_got):
    width = own.shape[0]
    return pl.pallas_call(
        product_kernel,
        out_shape=[
            jax.ShapeDtypeStruct(own.shape, BF16),
            jax.ShapeDtypeStruct(own.shape, BF16),
            jax.ShapeDtypeStruct(bias.shape, F32),
            jax.ShapeDtypeStruct((8, 128), F32),
        ],
        in_specs=[SMEM] + [VMEM] * 4,
        out_specs=[VMEM] * 4,
        compiler_params=room(14),
        cost_estimate=pl.CostEstimate(flops=2 * width**3, bytes_accessed=6 * width**2, transcendentals=0),
    )(core.reshape(1), own, got, bias, bias_got)


def hold_kernel(value, ready, out):
    out[...] = value[...]


def held(value, ready):
    return pl.pallas_call(
        hold_kernel,
        out_shape=jax.ShapeDtypeStruct(value.shape, value.dtype),
        in_specs=[VMEM, VMEM],
        out_specs=VMEM,
        compiler_params=SMALL,
    )(value, ready)


def join_kernel(a, b, ready, out):
    out[...] = a[...] + b[...]


def joined(a, b, ready):
    return pl.pallas_call(
        join_kernel,
        out_shape=jax.ShapeDtypeStruct(a.shape, a.dtype),
        in_specs=[VMEM, VMEM, VMEM],
        out_specs=VMEM,
        compiler_params=SMALL,
        cost_estimate=pl.CostEstimate(flops=4 * 10**10, bytes_accessed=0, transcendentals=0),
    )(a, b, ready)


def settle_kernel(flags, entry, relayed, last, edge, out):
    @pl.when(flags[1] != 0)
    def _():
        out[...] = entry[...] + relayed[...] + last[...]

    @pl.when(flags[1] == 0)
    def _():
        out[...] = edge[...]


def settled(flags, entry, relayed, last, edge):
    return pl.pallas_call(
        settle_kernel,
        out_shape=jax.ShapeDtypeStruct(entry.shape, entry.dtype),
        in_specs=[SMEM] + [VMEM] * 4,
        out_specs=VMEM,
        compiler_params=SMALL,
    )(flags, entry, relayed, last, edge)


def close_kernel(flags, maps, entry, across, other, v_odd, out):
    low, below = flags[0] != 0, flags[1] != 0

    @pl.when(low & below)
    def _():
        out[...] = mm(across[...], maps[...]) + other[...].astype(F32)

    @pl.when(low & jnp.logical_not(below))
    def _():
        out[...] = across[...].astype(F32)

    @pl.when(jnp.logical_not(low) & below)
    def _():
        out[...] = mm(entry[...], maps[...]) + v_odd[...]

    @pl.when(jnp.logical_not(low) & jnp.logical_not(below))
    def _():
        out[...] = v_odd[...]


def closed(flags, maps, entry, across, other, v_odd):
    return pl.pallas_call(
        close_kernel,
        out_shape=jax.ShapeDtypeStruct(entry.shape, F32),
        in_specs=[SMEM] + [VMEM] * 5,
        out_specs=VMEM,
        compiler_params=room(5),
    )(flags, maps, entry, across, other, v_odd)


def body(inv_diag, couple, arrow, corner, band_offset):
    depth_count = lax.axis_size("depth")
    lat_count = lax.axis_size("lat")
    depth = lax.axis_index("depth")
    lat = lax.axis_index("lat")
    core = depth % 2
    chip = depth // 2
    chips = depth_count // 2
    low = core == 0
    y, x = lat // SIDE, lat % SIDE
    order = [
        jnp.where(low, SIDE * b + a, SIDE * a + b)
        for b in around(jnp.where(low, y, x))
        for a in around(jnp.where(low, x, y))
    ]
    g_rows = inv_diag[0]
    share, width = g_rows.shape
    cells = couple[0].T
    row = lax.broadcasted_iota(jnp.int32, cells.shape, 0) + lat * share
    col = lax.broadcasted_iota(jnp.int32, cells.shape, 1)
    keep = jnp.abs(row - col - band_offset[0]) <= HALF
    pair = jnp.stack([g_rows, jnp.where(keep, cells, jnp.zeros_like(cells))])
    panel = mm(corner, arrow[0]).astype(BF16).reshape(lat_count, 2, share // 2, share)
    panel = jnp.swapaxes(panel, 1, 2).reshape(lat_count, share // 2, 2 * share)
    panel_rows = lax.all_to_all(panel, "lat", 0, 0)
    everyone = range(depth_count)
    first = pack(ring_gather(pair, everyone, False))
    blocks = ring_gather(first, everyone, True)
    order = jnp.stack(order)
    step, bias = step_terms(order, panel_rows, blocks)
    swap = [(d, d ^ 1) for d in range(depth_count)]
    got = lax.ppermute(step, "depth", swap)
    bias_got = lax.ppermute(bias, "depth", [(2 * k, 2 * k + 1) for k in range(chips)])
    product, step_odd, add_even, turn = products(core, step, got, bias, bias_got)
    add_odd = jnp.where(low, jnp.zeros_like(bias), bias)
    lower = (chips * 6) // 16
    tops = [chips - 1, lower - 1]
    sizes = [chips - lower, lower]
    start = (row == col) & ((chip == tops[0]) | (chip == tops[1])) & low
    v_in = jnp.where(start, 1.0, 0.0).astype(BF16)
    v_in = held(v_in, sent_down(turn, [(k + 1, k) for k in range(lower)]))
    v_even = mm(v_in, product) + add_even
    for hop in range(1, max(sizes)):
        pairs = []
        for block_top, size, cores in zip(tops, sizes, ((1,), (0, 1))):
            if hop < size:
                source = block_top - hop + 1
                pairs += [(2 * source + k, 2 * source - 2 + k) for k in cores]
        v_in = v_in + lax.ppermute(v_even.astype(BF16), "depth", pairs)
        v_even = mm(v_in, product) + add_even
    edge = v_even.astype(BF16)
    v_odd = mm(v_in, step_odd) + add_odd
    other = lax.ppermute(
        jnp.where(low, v_odd.astype(BF16), edge), "depth", swap[: 2 * lower]
    )
    map_rows = jnp.where(low, edge, other)
    depths = range(2 * lower)
    ring = jnp.concatenate(ring_gather(map_rows, depths, False))
    near, far = lower - 1, lower // 2 - 1
    to_far = sent_down(edge, [(lower, far)])
    entry = joined(to_far, sent_down(edge, [(lower, near)]), ring)
    relayed = sent_down(entry, [(near, near - 1), (far, far - 1)])
    last = [(source, source - 2) for source, low_end in ((near, far), (far, -1)) if source - 2 > low_end]
    last = sent_down(entry, last)
    maps = place(order, ring_gather(ring, depths, True))
    below = chip < lower
    flags = jnp.stack([low, below]).astype(jnp.int32)
    entry = settled(flags, entry, relayed, last, edge)
    across = lax.ppermute(entry, "depth", [(2 * k + 1, 2 * k) for k in range(chips)])
    return closed(flags, maps, entry, across, other, v_odd)[None]


def solution(mesh):
    placed = (
        P("depth", "lat", None),
        P("depth", None, "lat"),
        P("depth", None, "lat"),
        P(),
        P("depth"),
    )
    return jax.shard_map(
        body, mesh=mesh, in_specs=placed, out_specs=P("depth", "lat", None), check_vma=False
    )
```
